256 devices in a mesh: lat: 4 (over y), lon: 32 (over x_hi, z, core), grp: 2 (over x_lo).
Axes of the slice: x: 4 (x_hi: 2, x_lo: 2; x = x_hi * 2 + x_lo), y: 4, z: 8, core: 2. Of those that a mesh axis runs over, the one named last changes fastest.
Arguments:
- fine_tokens: bfloat16 [4, 24, 768, 512], P('grp', 'lat', 'lon'), may hold values from -16 to 16
- region_ids: int32 [4, 24, 768], P('grp', 'lat', 'lon'), may hold values from 0 to 9, as said below
- inward_weight: bfloat16 [512, 1536], replicated, may hold values from -2.5 to 2.5
- outward_weight: bfloat16 [512, 512], replicated, may hold values from -0.25 to 0.25
- merging_weight: bfloat16 [2048, 1024], replicated, may hold values from -0.125 to 0.125
- coarse_cotangent: bfloat16 [4, 12, 384, 1024], P('grp', 'lat', 'lon'), may hold values from -6 to 6
Outputs:
- coarse_field: bfloat16 [4, 12, 384, 1024], P('grp', 'lat', 'lon')
- token_grads: bfloat16 [4, 24, 768, 512], P('grp', 'lat', 'lon')
- inward_grads: float32 [512, 1536], P(None, 'lon')
- outward_grads: float32 [512, 512], P(None, 'lon')
- merging_grads: float32 [2048, 1024], P(None, 'lon')
The draws below stay inside these ranges and needn't reach their ends.
Inputs may be any that keep to these rules, and one draw needn't show every extreme that they name: `region_ids`: region label of each position of the rolled grid; a query attends only to keys of its own label.
All inputs are finite; a program needn't handle non-finite values.
Results may differ from the reference program's by a relative error of at most 0.02.
Values may be sent and summed in bfloat16 or wider, within the bound.
No kernel may reach another device: no remote copies, remote signals or barrier semaphores. Data moves between devices by JAX's collectives and lax.ppermute only.
A program may use at most 128 MiB of HBM per device.

```python
import jax
import jax.numpy as jnp
from jax import lax

FINE = 512
COARSE = 1024
HEADS = 16
WIN_LEV = 2
WIN_LAT = 6
WIN_LON = 12
LEVELS = 4
LAT_ROWS = 24
LON_COLS = 768


def draw_fine_tokens(key, part):
    key = jax.random.fold_in(key, 5)
    full_shape = (LEVELS, LAT_ROWS, LON_COLS, FINE)
    base_key = jax.random.fold_in(key, 0)
    values = jnp.clip(jax.random.normal(base_key, full_shape, jnp.float32), -6.0, 6.0)
    return values.astype(jnp.bfloat16)


def draw_inward_weight(key, part):
    key = jax.random.fold_in(key, 7)
    full_shape = (FINE, 3 * FINE)
    spread = FINE ** (-0.5)
    noise_key = jax.random.fold_in(key, 0)
    values = jax.random.normal(noise_key, full_shape, jnp.float32) * spread
    return values.astype(jnp.bfloat16)


def draw_region_ids(key, part):
    key = jax.random.fold_in(key, 11)
    level_key, row_key, column_key = jax.random.split(key, 3)
    full_shape = (LEVELS, LAT_ROWS, LON_COLS)
    level_index = lax.broadcasted_iota(jnp.int32, full_shape, 0)
    row_index = lax.broadcasted_iota(jnp.int32, full_shape, 1)
    column_index = lax.broadcasted_iota(jnp.int32, full_shape, 2)
    level_region = (level_index >= LEVELS - WIN_LEV).astype(jnp.int32) + (level_index >= LEVELS - WIN_LEV // 2).astype(jnp.int32)
    row_region = (row_index >= LAT_ROWS - WIN_LAT).astype(jnp.int32) + (row_index >= LAT_ROWS - WIN_LAT // 2).astype(jnp.int32)
    labels = 3 * level_region + row_region
    level_pick = jax.random.randint(level_key, (), 0, LEVELS)
    row_pick = jax.random.randint(row_key, (), 0, LAT_ROWS)
    column_pick = jax.random.randint(column_key, (), 0, LON_COLS)
    partner = jnp.bitwise_xor(column_pick, 1)
    pair_cells = (level_index == level_pick) & (row_index == row_pick) & ((column_index == column_pick) | (column_index == partner))
    return jnp.where(pair_cells, 9, labels).astype(jnp.int32)


def with_spikes(drawn, key, source, target, parts, factor):
    def block_of(position):
        return (jnp.arange(drawn.shape[position]) // (drawn.shape[position] // parts)).reshape((-1,) + (1,) * (drawn.ndim - 1 - position))

    near = jax.random.permutation(key, parts)[block_of(target)]
    second = (block_of(target) + parts // 2) % parts
    return jnp.where((block_of(source) == near) | (block_of(source) == second), factor * drawn, drawn)


def block_levels(stream_key, extent, pieces, least, largest):
    def one(axis_at, shards_of):
        steps = jax.random.uniform(jax.random.fold_in(jax.random.fold_in(stream_key, 6), axis_at), (shards_of,), jnp.float32, least / len(pieces), largest / len(pieces))
        return jnp.repeat(jnp.exp(steps), extent[axis_at] // shards_of).reshape((-1,) + (1,) * (len(extent) - axis_at - 1))

    factor_of = one(*pieces[0])
    for cut in pieces[1:]:
        factor_of = factor_of * one(*cut)
    return factor_of


def gaussian(stream_key, extent, deviation, bound, cuts=(), kind=jnp.bfloat16):
    array = deviation * jax.random.normal(stream_key, extent, jnp.float32)
    if cuts:
        array = array * block_levels(stream_key, extent, cuts, -0.22, 0.18)
    return jnp.clip(array, -bound, bound).astype(kind)


def heavy_noise(key, extent, deviation, bound, cuts, heavy, dtype=jnp.bfloat16):
    values = deviation * jax.random.normal(key, extent, jnp.float32)
    if cuts:
        values = values * block_levels(key, extent, cuts, -0.22, 0.18)
    return jnp.clip(with_spikes(values, jax.random.fold_in(key, 3), *heavy), -bound, bound).astype(dtype)


def setup_inputs(seed: int = 0) -> dict:
    splits = jax.random.split(jax.random.key(seed), 7)
    return {
        "fine_tokens": draw_fine_tokens(jax.random.fold_in(splits[6], 71), 0),
        "region_ids": draw_region_ids(jax.random.fold_in(splits[6], 71), 0),
        "inward_weight": draw_inward_weight(jax.random.fold_in(splits[6], 71), 0),
        "outward_weight": gaussian(splits[3], (FINE, FINE), FINE ** -0.5, 0.25),
        "merging_weight": gaussian(splits[4], (4 * FINE, COARSE), (4 * FINE) ** -0.5, 0.125),
        "coarse_cotangent": heavy_noise(splits[5], (LEVELS, LAT_ROWS // 2, LON_COLS // 2, COARSE), 1.0, 6.0, ((0, 2), (1, 4), (2, 32)), (2, 3, 32, 2.75)),
    }


def layer_norm(values):
    centred = values - lax.optimization_barrier(jnp.mean(values, axis=-1, keepdims=True))
    inverse_std = lax.rsqrt(lax.optimization_barrier(jnp.mean(centred * centred, axis=-1, keepdims=True)) + 1e-05)
    return (centred * inverse_std, inverse_std)

def norm_back(upstream, normalized, inverse_std):
    return inverse_std * (upstream - lax.optimization_barrier(jnp.mean(upstream, axis=-1, keepdims=True)) - normalized * lax.optimization_barrier(jnp.mean(upstream * normalized, axis=-1, keepdims=True)))

def merge_patches(layout):
    level_count, row_count, column_count, channel_count = layout.shape
    blocks = layout.reshape(level_count, row_count // 2, 2, column_count // 2, 2, channel_count)
    blocks = jnp.transpose(blocks, (0, 1, 3, 4, 2, 5))
    return blocks.reshape(level_count, row_count // 2, column_count // 2, 4 * channel_count)

def split_patches(merged):
    level_count, half_rows, half_columns, merged_width = merged.shape
    blocks = merged.reshape(level_count, half_rows, half_columns, 2, 2, merged_width // 4)
    blocks = jnp.transpose(blocks, (0, 1, 4, 2, 3, 5))
    return blocks.reshape(level_count, 2 * half_rows, 2 * half_columns, merged_width // 4)

def global_windows(layout):
    level_count, row_count, column_count = layout.shape[:3]
    trailing = layout.shape[3:]
    blocks = layout.reshape((level_count // WIN_LEV, WIN_LEV, row_count // WIN_LAT, WIN_LAT, column_count // WIN_LON, WIN_LON) + trailing)
    axes_order = (0, 2, 4, 1, 3, 5) + tuple(range(6, 6 + len(trailing)))
    blocks = jnp.transpose(blocks, axes_order)
    return blocks.reshape((level_count // WIN_LEV * (row_count // WIN_LAT), column_count // WIN_LON, WIN_LEV * WIN_LAT * WIN_LON) + trailing)

def global_fields(windows, level_count, row_count, column_count):
    trailing = windows.shape[3:]
    blocks = windows.reshape((level_count // WIN_LEV, row_count // WIN_LAT, column_count // WIN_LON, WIN_LEV, WIN_LAT, WIN_LON) + trailing)
    axes_order = (0, 3, 1, 4, 2, 5) + tuple(range(6, 6 + len(trailing)))
    blocks = jnp.transpose(blocks, axes_order)
    return blocks.reshape((level_count, row_count, column_count) + trailing)

def window_forward(windows, labels, inward_weight, outward_weight):
    window_count, token_count, channel_count = windows.shape
    score_scale = (channel_count // HEADS) ** (-0.5)
    normed_exact, inverse_std = layer_norm(windows.astype(jnp.float32))
    normed = normed_exact.astype(jnp.bfloat16)
    projected = jnp.dot(normed, inward_weight, preferred_element_type=jnp.float32).astype(jnp.bfloat16)
    split_heads = projected.reshape(window_count, token_count, 3, HEADS, channel_count // HEADS)
    query_heads = split_heads[:, :, 0]
    key_heads = split_heads[:, :, 1]
    value_heads = split_heads[:, :, 2]
    scores = jnp.einsum('wqhd,wkhd->whqk', query_heads.astype(jnp.float32), key_heads.astype(jnp.float32)) * score_scale
    allowed = (labels[:, :, None] == labels[:, None, :])[:, None]
    scores = jnp.where(allowed, scores, -1e+30)
    highest = lax.optimization_barrier(jnp.max(scores, axis=-1, keepdims=True))
    weights = jnp.exp(scores - highest)
    attention = weights / lax.optimization_barrier(jnp.sum(weights, axis=-1, keepdims=True))
    attention_low = attention.astype(jnp.bfloat16)
    attended = jnp.einsum('whqk,wkhd->wqhd', attention_low.astype(jnp.float32), value_heads.astype(jnp.float32)).astype(jnp.bfloat16)
    attended = attended.reshape(window_count, token_count, channel_count)
    branch = jnp.dot(attended, outward_weight, preferred_element_type=jnp.float32)
    result = (windows.astype(jnp.float32) + branch).astype(jnp.bfloat16)
    stored = (normed_exact, inverse_std, normed, query_heads, key_heads, value_heads, attention, attention_low, attended)
    return (result, stored)

def window_backward(upstream, stored, inward_weight, outward_weight):
    normed_exact, inverse_std, normed, query_heads, key_heads, value_heads, attention, attention_low, attended = stored
    window_count, token_count, channel_count = upstream.shape
    score_scale = (channel_count // HEADS) ** (-0.5)
    outward_term = jnp.einsum('wtc,wtd->cd', attended.astype(jnp.float32), upstream.astype(jnp.float32))
    attended_back = jnp.einsum('wtd,cd->wtc', upstream.astype(jnp.float32), outward_weight.astype(jnp.float32)).astype(jnp.bfloat16)
    attended_back = attended_back.reshape(window_count, token_count, HEADS, channel_count // HEADS)
    attention_back = jnp.einsum('wqhd,wkhd->whqk', attended_back.astype(jnp.float32), value_heads.astype(jnp.float32))
    value_back = jnp.einsum('whqk,wqhd->wkhd', attention_low.astype(jnp.float32), attended_back.astype(jnp.float32))
    score_back = attention * (attention_back - lax.optimization_barrier(jnp.sum(attention * attention_back, axis=-1, keepdims=True)))
    score_back = (score_back * score_scale).astype(jnp.bfloat16)
    query_back = jnp.einsum('whqk,wkhd->wqhd', score_back.astype(jnp.float32), key_heads.astype(jnp.float32))
    key_back = jnp.einsum('whqk,wqhd->wkhd', score_back.astype(jnp.float32), query_heads.astype(jnp.float32))
    projected_back = jnp.stack([query_back, key_back, value_back], axis=2)
    projected_back = projected_back.reshape(window_count, token_count, 3 * channel_count).astype(jnp.bfloat16)
    inward_term = jnp.einsum('wtc,wtd->cd', normed.astype(jnp.float32), projected_back.astype(jnp.float32))
    normed_back = jnp.einsum('wtd,cd->wtc', projected_back.astype(jnp.float32), inward_weight.astype(jnp.float32))
    branch_back = norm_back(normed_back, normed_exact, inverse_std).astype(jnp.bfloat16)
    return (branch_back, inward_term, outward_term)

def reference(fine_tokens, region_ids, inward_weight, outward_weight, merging_weight, coarse_cotangent):
    offsets = (WIN_LEV // 2, WIN_LAT // 2, WIN_LON // 2)
    negative = (-offsets[0], -offsets[1], -offsets[2])
    level_count, row_count, column_count, channel_count = fine_tokens.shape
    rolled = jnp.roll(fine_tokens, negative, axis=(0, 1, 2))
    windows = global_windows(rolled)
    labels = global_windows(region_ids)

    def forward_row(row_pair):
        return window_forward(row_pair[0], row_pair[1], inward_weight, outward_weight)[0]
    block_rolled = lax.map(forward_row, (windows, labels))
    block_out = jnp.roll(global_fields(block_rolled, level_count, row_count, column_count), offsets, axis=(0, 1, 2))
    merged = merge_patches(block_out)
    merged_exact, merged_inverse = layer_norm(merged.astype(jnp.float32))
    merged_normed = merged_exact.astype(jnp.bfloat16)
    coarse_field = jnp.dot(merged_normed, merging_weight, preferred_element_type=jnp.float32).astype(jnp.bfloat16)
    flat_normed = merged_normed.reshape(-1, 4 * channel_count)
    flat_cotangent = coarse_cotangent.reshape(-1, coarse_cotangent.shape[-1])
    merging_grads = jnp.dot(flat_normed.T, flat_cotangent, preferred_element_type=jnp.float32)
    merged_upstream = jnp.einsum('abcy,xy->abcx', coarse_cotangent.astype(jnp.float32), merging_weight.astype(jnp.float32))
    merged_back = norm_back(merged_upstream, merged_exact, merged_inverse).astype(jnp.bfloat16)
    block_back = split_patches(merged_back)
    upstream = global_windows(jnp.roll(block_back, negative, axis=(0, 1, 2)))

    def backward_row(totals, triple):
        row_windows, row_labels, row_upstream = triple
        stored = window_forward(row_windows, row_labels, inward_weight, outward_weight)[1]
        branch_back, inward_term, outward_term = window_backward(row_upstream, stored, inward_weight, outward_weight)
        return ((totals[0] + inward_term, totals[1] + outward_term), branch_back)
    start = (jnp.zeros((channel_count, 3 * channel_count), jnp.float32), jnp.zeros((channel_count, channel_count), jnp.float32))
    sums, branch_back = lax.scan(backward_row, start, (windows, labels, upstream))
    inward_grads, outward_grads = sums
    branch_layout = jnp.roll(global_fields(branch_back, level_count, row_count, column_count), offsets, axis=(0, 1, 2))
    token_grads = (block_back.astype(jnp.float32) + branch_layout.astype(jnp.float32)).astype(jnp.bfloat16)
    return (coarse_field, token_grads, inward_grads, outward_grads, merging_grads)
```

```python
import jax
import jax.numpy as jnp
import numpy as np
from jax import lax
from jax.experimental import pallas as pl
from jax.experimental.pallas import tpu as pltpu
from jax.sharding import Mesh, PartitionSpec as P

HEADS = 16
LON = ("xh", "z", "core")
SCALE = 32 ** (-0.5)
LOW = jnp.bfloat16
WIDE = jnp.float32


def token_maps():
    natural = np.arange(288).reshape(2, 6, 24)
    windows = natural.reshape(2, 6, 2, 12).transpose(2, 0, 1, 3).reshape(288)
    to_windows = np.eye(288, dtype=np.float32)[windows]
    extended = np.concatenate([288 + np.arange(48).reshape(2, 1, 24), natural[:, :5]], axis=1)
    cells = extended.reshape(2, 3, 2, 12, 2).transpose(4, 2, 0, 1, 3).reshape(288)
    to_cells = np.eye(336, dtype=np.float32)[cells]
    last_row = np.zeros((288, 48), np.float32)
    last_row[natural[:, 5].reshape(48), np.arange(48)] = 1.0
    return (to_windows, to_cells, to_windows @ last_row)


TO_WINDOWS, TO_CELLS, LAST_ROW = token_maps()


def dot_nn(a, b):
    return lax.dot_general(a, b, (((1,), (0,)), ((), ())), preferred_element_type=WIDE)


def dot_nt(a, b):
    return lax.dot_general(a, b, (((1,), (1,)), ((), ())), preferred_element_type=WIDE)


def dot_tn(a, b):
    return lax.dot_general(a, b, (((0,), (0,)), ((), ())), preferred_element_type=WIDE)


def head_masks():
    head = lax.broadcasted_iota(jnp.int32, (144, 128), 1) >> 5
    return [(head == h).astype(WIDE).astype(LOW) for h in range(4)]


def normalize(values):
    centred = values - jnp.mean(values, axis=-1, keepdims=True)
    inverse_std = lax.rsqrt(jnp.mean(centred * centred, axis=-1, keepdims=True) + 1e-05)
    return (centred * inverse_std, inverse_std)


def forward_kernel(
    tokens, row_labels, column_labels, to_windows, from_windows, inward, outward,
    block, windows, projected, attention, attended,
):
    values = dot_nn(to_windows[...], tokens[...])
    windows[...] = values.astype(LOW)
    normed = normalize(values)[0].astype(LOW)
    projected[...] = dot_nn(normed, inward[...]).astype(LOW)
    masks = head_masks()
    for w in range(2):
        rows = slice(144 * w, 144 * w + 144)
        allowed = column_labels[w] == row_labels[w]
        for t in range(4):
            query = projected[rows, 128 * t : 128 * t + 128]
            key = projected[rows, 512 + 128 * t : 640 + 128 * t]
            value_t = projected[rows, 1024 + 128 * t : 1152 + 128 * t].T
            parts = []
            for h in range(4):
                scores = dot_nt(key * masks[h], query) * SCALE
                scores = jnp.where(allowed, scores, -1e30)
                weights = jnp.exp(scores - jnp.max(scores, axis=0, keepdims=True))
                share = weights * (1.0 / jnp.sum(weights, axis=0, keepdims=True))
                share = share.astype(LOW)
                attention[w, 4 * t + h] = share
                parts.append(dot_nn(value_t[32 * h : 32 * h + 32], share))
            attended[rows, 128 * t : 128 * t + 128] = jnp.concatenate(parts, axis=0).T.astype(LOW)
    result = (values + dot_nn(attended[...], outward[...])).astype(LOW)
    block[...] = dot_nn(from_windows[...], result).astype(LOW)


def merge_kernel(block, prior, to_cells, from_cells, upstream, normed, back, back_row):
    merged = dot_nn(to_cells[:, :288], block[...]) + dot_nn(to_cells[:, 288:], prior[...])
    pieces = [merged[72 * k : 72 * k + 72] for k in range(4)]
    exact, inverse_std = normalize(jnp.concatenate(pieces, axis=1))
    normed[...] = exact.astype(LOW)
    grads = upstream[...]
    grads = inverse_std * (
        grads
        - jnp.mean(grads, axis=-1, keepdims=True)
        - exact * jnp.mean(grads * exact, axis=-1, keepdims=True)
    )
    stacked = jnp.concatenate([grads[:, 512 * k : 512 * k + 512] for k in range(4)], axis=0)
    stacked = stacked.astype(LOW)
    back[...] = dot_nn(from_cells[:288], stacked).astype(LOW)
    back_row[...] = dot_nn(from_cells[288:], stacked).astype(LOW)


def coarse_kernel(normed, cotangent, weight, coarse, terms):
    coarse[...] = dot_nn(normed[...], weight[...]).astype(LOW)
    for j in range(8):
        chunk = dot_tn(cotangent[:, 128 * j : 128 * j + 128], normed[...]).astype(LOW)
        for i in range(4):
            place = 4 * j + i
            for k in range(8):
                terms[place % 2, place // 16, k // 2, k % 2, place // 2 % 8] = chunk[
                    32 * i : 32 * i + 32, 256 * k : 256 * k + 256
                ]


def backward_kernel(
    back, next_row, windows, projected, attention, attended, to_windows, last_row, from_windows, inward, outward,
    token_grads, terms, projected_back,
):
    upstream = dot_nn(to_windows[...], back[...]) + dot_nn(last_row[...], next_row[...])
    upstream_low = upstream.astype(LOW)
    attended_back = dot_nt(upstream_low, outward[...]).astype(LOW)
    masks = head_masks()
    for w in range(2):
        rows = slice(144 * w, 144 * w + 144)
        for t in range(4):
            query = projected[rows, 128 * t : 128 * t + 128]
            key_t = projected[rows, 512 + 128 * t : 640 + 128 * t].T
            value = projected[rows, 1024 + 128 * t : 1152 + 128 * t]
            grads = attended_back[rows, 128 * t : 128 * t + 128]
            query_parts, key_back, value_back = [], 0.0, 0.0
            for h in range(4):
                low = attention[w, 4 * t + h]
                share = low.astype(WIDE)
                product = share * dot_nt(value * masks[h], grads)
                total = jnp.sum(product, axis=0, keepdims=True)
                score_back = ((product - share * total) * SCALE).astype(LOW)
                value_back += dot_nn(low, grads * masks[h])
                key_back += dot_nn(score_back, query * masks[h])
                query_parts.append(dot_nn(key_t[32 * h : 32 * h + 32], score_back))
            query_back = jnp.concatenate(query_parts, axis=0).T
            projected_back[rows, 128 * t : 128 * t + 128] = query_back.astype(LOW)
            projected_back[rows, 512 + 128 * t : 640 + 128 * t] = key_back.astype(LOW)
            projected_back[rows, 1024 + 128 * t : 1152 + 128 * t] = value_back.astype(LOW)
    normed, inverse_std = normalize(windows[...].astype(WIDE))
    normed_low = normed.astype(LOW)
    for j in range(4):
        inward_t = dot_tn(projected_back[:, 384 * j : 384 * j + 384], normed_low).astype(LOW)
        outward_t = dot_tn(upstream_low[:, 128 * j : 128 * j + 128], attended[...]).astype(LOW)
        for i in range(8):
            place = 8 * j + i
            for k in range(4):
                lanes = slice(128 * k, 128 * k + 128)
                at = (place % 2, place // 16, k)
                terms[at + (0, place // 2 % 8)] = inward_t[48 * i : 48 * i + 32, lanes]
                terms[at + (1, place // 2 % 8, slice(0, 16))] = inward_t[48 * i + 32 : 48 * i + 48, lanes]
                terms[at + (1, place // 2 % 8, slice(16, 32))] = outward_t[16 * i : 16 * i + 16, lanes]
    normed_back = dot_nt(projected_back[...], inward[...])
    branch = inverse_std * (
        normed_back
        - jnp.mean(normed_back, axis=-1, keepdims=True)
        - normed * jnp.mean(normed_back * normed, axis=-1, keepdims=True)
    )
    result = (upstream + branch.astype(LOW).astype(WIDE)).astype(LOW)
    token_grads[...] = dot_nn(from_windows[...], result).astype(LOW)


def call(kernel, outs, *operands, scratch=()):
    return pl.pallas_call(
        kernel,
        out_shape=[jax.ShapeDtypeStruct(shape, LOW) for shape in outs],
        scratch_shapes=[pltpu.VMEM(shape, LOW) for shape in scratch],
        compiler_params=pltpu.CompilerParams(vmem_limit_bytes=48 * 1024 * 1024),
    )(*operands)


def from_behind(value, axis, steps):
    count = lax.axis_size(axis)
    pairs = [(source, (source + steps) % count) for source in range(count)]
    return lax.ppermute(value, axis, pairs)


def local_windows(layout):
    return layout.reshape(2, 6, 2, 12).transpose(2, 0, 1, 3).reshape(2, 144)


def roll_forward(layout, levels, rows, columns):
    level_next = from_behind(layout[:levels], ("grp",), -1)
    layout = jnp.concatenate([layout[levels:], level_next], axis=0)
    row_next = from_behind(layout[:, :rows], ("lat",), -1)
    layout = jnp.concatenate([layout[:, rows:], row_next], axis=1)
    column_next = from_behind(layout[:, :, :columns], LON, -1)
    return jnp.concatenate([layout[:, :, columns:], column_next], axis=2)


def roll_back(layout, levels, rows, columns):
    column_prior = from_behind(layout[:, :, -columns:], LON, 1)
    layout = jnp.concatenate([column_prior, layout[:, :, :-columns]], axis=2)
    row_prior = from_behind(layout[:, -rows:], ("lat",), 1)
    layout = jnp.concatenate([row_prior, layout[:, :-rows]], axis=1)
    level_prior = from_behind(layout[-levels:], ("grp",), 1)
    return jnp.concatenate([level_prior, layout[:-levels]], axis=0)


def wide_sum(parts):
    return jnp.sum(parts.astype(WIDE), axis=0).astype(LOW)


def over_planes(terms):
    core = lax.axis_index("core")
    sent = lax.dynamic_index_in_dim(terms, 1 - core, 0, keepdims=False)
    kept = lax.dynamic_index_in_dim(terms, core, 0, keepdims=False)
    came = from_behind(sent, ("core",), 1)
    summed = (kept.astype(WIDE) + came.astype(WIDE)).astype(LOW)
    summed = summed.reshape((16,) + terms.shape[4:])
    return wide_sum(lax.all_to_all(summed, ("xh", "lat", "grp"), 0, 0))


def body(fine_tokens, region_ids, inward_weight, outward_weight, merging_weight, coarse_cotangent):
    to_windows = jnp.asarray(TO_WINDOWS, LOW)
    from_windows = jnp.asarray(TO_WINDOWS.T, LOW)
    to_cells = jnp.asarray(TO_CELLS, LOW)
    from_cells = jnp.asarray(TO_CELLS.T, LOW)
    last_row = jnp.asarray(LAST_ROW, LOW)
    rolled = roll_forward(fine_tokens, 1, 3, 6).reshape(288, 512)
    cotangent = roll_forward(coarse_cotangent, 1, 1, 3).reshape(72, 1024)
    labels = local_windows(region_ids)
    block, windows, projected, attention, attended = call(
        forward_kernel,
        [(288, 512), (288, 512), (288, 1536), (2, HEADS, 144, 144), (288, 512)],
        rolled, labels.reshape(2, 1, 144), labels.reshape(2, 144, 1), to_windows, from_windows, inward_weight, outward_weight,
    )
    prior = from_behind(block.reshape(2, 6, 24, 512)[:, 5].reshape(48, 512), ("lat",), 1)
    merged_upstream = dot_nt(cotangent, merging_weight)
    merged_normed, back, back_row = call(
        merge_kernel,
        [(72, 2048), (288, 512), (48, 512)],
        block, prior, to_cells, from_cells, merged_upstream,
    )
    next_row = from_behind(back_row, ("lat",), -1)
    coarse_field, merging_terms = call(
        coarse_kernel,
        [(72, 1024), (2, 2, 4, 2, 8, 32, 256)],
        merged_normed, cotangent, merging_weight,
    )
    token_grads, block_terms = call(
        backward_kernel,
        [(288, 512), (2, 2, 4, 2, 8, 32, 128)],
        back, next_row, windows, projected, attention, attended,
        to_windows, last_row, from_windows, inward_weight, outward_weight,
        scratch=[(288, 1536)],
    )
    coarse_field = roll_back(coarse_field.reshape(2, 3, 12, 1024), 1, 1, 3)
    token_grads = roll_back(token_grads.reshape(2, 6, 24, 512), 1, 3, 6)
    planes = jnp.concatenate([over_planes(block_terms), over_planes(merging_terms)], axis=2)
    share = wide_sum(lax.all_to_all(planes, ("z",), 0, 0))
    shares = lax.all_to_all(jnp.broadcast_to(share[None], (8, 32, 384)), ("lat", "grp"), 0, 0)
    shares = shares.reshape(4, 2, 32, 384).astype(WIDE)
    block_grads = shares[..., :128].transpose(0, 3, 1, 2).reshape(512, 64)
    merging_grads = shares[..., 128:].transpose(0, 1, 3, 2).reshape(2048, 32)
    return (coarse_field, token_grads, block_grads[:, :48], block_grads[:, 48:], merging_grads)


def solution(mesh):
    fine = Mesh(mesh.devices.reshape(4, 2, 8, 2, 2), ("lat", "xh", "z", "core", "grp"))
    return jax.shard_map(
        body,
        mesh=fine,
        in_specs=(
            P("grp", "lat", LON, None),
            P("grp", "lat", LON),
            P(),
            P(),
            P(),
            P("grp", "lat", LON, None),
        ),
        out_specs=(
            P("grp", "lat", LON, None),
            P("grp", "lat", LON, None),
            P(None, LON),
            P(None, LON),
            P(None, LON),
        ),
        check_vma=False,
    )
```

```python
import jax
import jax.numpy as jnp
import numpy as np
from jax import lax
from jax.experimental import pallas as pl
from jax.experimental.pallas import tpu as pltpu
from jax.sharding import Mesh, PartitionSpec as P

HEADS = 16
LON = ("xh", "z", "core")
SCALE = 32 ** (-0.5)
LOW = jnp.bfloat16
WIDE = jnp.float32


def halves(fields):
    return np.concatenate([fields.reshape(-1), (fields + 1000).reshape(-1)])


def join(*parts):
    return np.concatenate([part.reshape(-1) for part in parts])


FINE_AT = np.arange(288).reshape(2, 6, 24)
CELL_AT = 1000 + np.arange(72).reshape(2, 3, 12)


def arrived(source, rows):
    fine = 1000 * source + np.arange(72).reshape(3, 24)
    cells = 1000 * source + 72 + np.arange(12 * rows).reshape(rows, 12)
    return fine, cells, 12 * rows


def shift_in():
    grp, lat, both = arrived(3, 2), arrived(4, 1), arrived(5, 1)
    first = [
        join(FINE_AT[0, 3:], halves(CELL_AT[0, 1:])),
        join(FINE_AT[1, :3], halves(CELL_AT[1, :1])),
        join(FINE_AT[0, :3], halves(CELL_AT[0, :1])),
    ]
    fine = np.stack([np.concatenate([FINE_AT[1, 3:], lat[0]]), np.concatenate([grp[0], both[0]])])
    left = np.stack([np.concatenate([CELL_AT[1, 1:], lat[1]]), np.concatenate([grp[1], both[1]])])
    right = np.stack(
        [np.concatenate([CELL_AT[1, 1:] + 1000, lat[1] + lat[2]]), np.concatenate([grp[1] + grp[2], both[1] + both[2]])]
    )
    second = join(fine[:, :, :6], left[:, :, :3], right[:, :, :3])
    lon_fine = 6000 + np.arange(72).reshape(2, 6, 6)
    lon_cells = 6072 + np.arange(18).reshape(2, 3, 3)
    fine = np.concatenate([fine[:, :, 6:], lon_fine], axis=2)
    left = np.concatenate([left[:, :, 3:], lon_cells], axis=2)
    right = np.concatenate([right[:, :, 3:], lon_cells + 18], axis=2)
    windows = fine.reshape(2, 6, 2, 12).transpose(2, 0, 1, 3)
    return join(*first), second, windows.reshape(-1), join(left, right)


def shift_out():
    first = join(FINE_AT[:, :, 18:], CELL_AT[:, :, 9:], CELL_AT[:, :, 9:] + 1000)
    lon_fine = 6000 + np.arange(72).reshape(2, 6, 6)
    lon_cells = 6072 + np.arange(18).reshape(2, 3, 3)
    fine = np.concatenate([lon_fine, FINE_AT[:, :, :18]], axis=2)
    left = np.concatenate([lon_cells, CELL_AT[:, :, :9]], axis=2)
    right = np.concatenate([lon_cells + 18, CELL_AT[:, :, :9] + 1000], axis=2)
    second = join(
        fine[1, :3], left[1, :2], right[1, :2], fine[0, 3:], left[0, 2], right[0, 2], fine[1, 3:], left[1, 2], right[1, 2]
    )
    grp, lat, both = arrived(3, 2), arrived(4, 1), arrived(5, 1)
    fine = np.stack([np.concatenate([both[0], grp[0]]), np.concatenate([lat[0], fine[0, :3]])])
    left = np.stack([np.concatenate([both[1], grp[1]]), np.concatenate([lat[1], left[0, :2]])])
    right = np.stack(
        [np.concatenate([both[1] + both[2], grp[1] + grp[2]]), np.concatenate([lat[1] + lat[2], right[0, :2]])]
    )
    return first, second, join(fine, left, right)


def block_maps():
    natural = np.arange(288).reshape(2, 6, 24)
    windows = natural.reshape(2, 6, 2, 12).transpose(2, 0, 1, 3).reshape(288)
    extended = np.concatenate([1000 + np.arange(48).reshape(2, 1, 24), natural[:, :5]], axis=1)
    to_cells = extended.reshape(2, 3, 2, 12, 2).transpose(4, 2, 0, 1, 3).reshape(288)
    from_cells = np.full(336, -1)
    from_cells[np.where(to_cells < 1000, to_cells, to_cells - 712)] = np.arange(288)
    replaced = natural.copy()
    replaced[:, 5] = 1000 + np.arange(48).reshape(2, 24)
    return np.argsort(windows), to_cells, from_cells, replaced.reshape(288)[windows]


def row_table():
    columns = [*shift_in(), *shift_out(), *block_maps()]
    table = np.full((432, len(columns)), -1, np.int32)
    for at, column in enumerate(columns):
        table[: len(column), at] = column
    return table


TABLE = row_table()
(
    IN_FIRST, IN_SECOND, IN_WINDOWS, IN_CELLS, OUT_FIRST, OUT_SECOND, OUT_ALL,
    FROM_WINDOWS, TO_CELLS, FROM_CELLS, UPSTREAM,
) = range(11)
ROWS = [int((TABLE[:, at] >= 0).sum()) for at in range(11)]
ROWS[FROM_CELLS] = 336


def gather(table, column, sources):
    names = table[: ROWS[column], column : column + 1]
    total = 0.0
    for source, value in sources.items():
        place = lax.broadcasted_iota(jnp.int32, (ROWS[column], value.shape[0]), 1) + 1000 * source
        total += dot_nn((names == place).astype(WIDE).astype(LOW), value)
    return total


def dot_nn(a, b):
    return lax.dot_general(a, b, (((1,), (0,)), ((), ())), preferred_element_type=WIDE)


def dot_nt(a, b):
    return lax.dot_general(a, b, (((1,), (1,)), ((), ())), preferred_element_type=WIDE)


def dot_tn(a, b):
    return lax.dot_general(a, b, (((0,), (0,)), ((), ())), preferred_element_type=WIDE)


def head_masks():
    head = lax.broadcasted_iota(jnp.int32, (144, 128), 1) >> 5
    return [(head == h).astype(WIDE).astype(LOW) for h in range(4)]


def normalize(values):
    centred = values - jnp.mean(values, axis=-1, keepdims=True)
    inverse_std = lax.rsqrt(jnp.mean(centred * centred, axis=-1, keepdims=True) + 1e-05)
    return (centred * inverse_std, inverse_std)


def own(tokens, cells):
    return {0: tokens[...], 1: cells[:, :512], 2: cells[:, 512:]}


def arrivals(grp, lat, both):
    return {3: grp[...], 4: lat[...], 5: both[...]}


def store_planes(packed, grp, lat, both):
    grp[...] = packed[:120].astype(LOW)
    lat[...] = packed[120:216].astype(LOW)
    both[...] = packed[216:].astype(LOW)


def planes_in_kernel(table, tokens, cells, *outs):
    store_planes(gather(table, IN_FIRST, own(tokens, cells)), *outs)


def columns_in_kernel(table, tokens, cells, grp, lat, both, out):
    out[...] = gather(table, IN_SECOND, own(tokens, cells) | arrivals(grp, lat, both)).astype(LOW)


def columns_out_kernel(table, tokens, cells, out):
    out[...] = gather(table, OUT_FIRST, own(tokens, cells)).astype(LOW)


def planes_out_kernel(table, tokens, cells, lon, *outs):
    store_planes(gather(table, OUT_SECOND, own(tokens, cells) | {6: lon[...]}), *outs)


def all_out_kernel(table, tokens, cells, grp, lat, both, lon, fine, coarse):
    packed = gather(table, OUT_ALL, own(tokens, cells) | arrivals(grp, lat, both) | {6: lon[...]})
    fine[...] = packed[:288].astype(LOW)
    coarse[:, :512] = packed[288:360].astype(LOW)
    coarse[:, 512:] = packed[360:].astype(LOW)


def shift_cotangent(core, table, sources, shifted, kept, sent, columns, picked):
    packed = gather(table, IN_CELLS, sources)
    cotangent = jnp.concatenate([packed[:72], packed[72:]], axis=1)
    shifted[...] = cotangent.astype(LOW)
    columns[...] = cotangent.T.astype(LOW)
    for out, parity in ((kept, core[0]), (sent, 1 - core[0])):
        for g in range(2):
            for m in range(16):
                at = pl.multiple_of(64 * m + 32 * parity + 16 * g, 16)
                picked[16 * m : 16 * m + 16] = columns[pl.ds(at, 16)]
            out[g] = picked[...].astype(WIDE).T.astype(LOW)


def forward_kernel(
    core, table, tokens, cells, grp, lat, both, lon, row_labels, column_labels, far_inward, far_outward,
    block, last_row, windows, projected, far_attention, attended, shifted, kept, sent,
    inward, outward, attention, columns, picked, weights_in, shares_out,
):
    fetches = [
        pltpu.make_async_copy(far_inward, inward, weights_in.at[0]),
        pltpu.make_async_copy(far_outward, outward, weights_in.at[1]),
    ]
    for copy in fetches:
        copy.start()
    stores = []
    arrived_parts = arrivals(grp, lat, both) | {6: lon[...]}
    values = gather(table, IN_WINDOWS, {0: tokens[...]} | arrived_parts)
    windows[...] = values.astype(LOW)
    normed = normalize(values)[0].astype(LOW)
    fetches[0].wait()
    projected[...] = dot_nn(normed, inward[...]).astype(LOW)
    masks = head_masks()
    for w in range(2):
        rows = slice(144 * w, 144 * w + 144)
        allowed = column_labels[w] == row_labels[w]
        for t in range(4):
            query = projected[rows, 128 * t : 128 * t + 128]
            key = projected[rows, 512 + 128 * t : 640 + 128 * t]
            value_t = projected[rows, 1024 + 128 * t : 1152 + 128 * t].T
            parts = []
            for h in range(4):
                scores = dot_nt(key * masks[h], query) * SCALE
                scores = jnp.where(allowed, scores, -1e30)
                weights = jnp.exp(scores - jnp.max(scores, axis=0, keepdims=True))
                share = weights * (1.0 / jnp.sum(weights, axis=0, keepdims=True))
                share = share.astype(LOW)
                attention[w, 4 * t + h] = share
                parts.append(dot_nn(value_t[32 * h : 32 * h + 32], share))
            attended[rows, 128 * t : 128 * t + 128] = jnp.concatenate(parts, axis=0).T.astype(LOW)
            heads = pl.ds(4 * t, 4)
            store = pltpu.make_async_copy(attention.at[w, heads], far_attention.at[w, heads], shares_out.at[w, t])
            store.start()
            stores.append(store)
    fetches[1].wait()
    result = (values + dot_nn(attended[...], outward[...])).astype(LOW)
    natural = gather(table, FROM_WINDOWS, {0: result})
    block[...] = natural.astype(LOW)
    last_row[...] = jnp.concatenate([natural[120:144], natural[264:]], axis=0).astype(LOW)
    cell_parts = {1: cells[:, :512], 2: cells[:, 512:]} | arrived_parts
    shift_cotangent(core, table, cell_parts, shifted, kept, sent, columns, picked)
    for store in stores:
        store.wait()


def merge_kernel(table, block, prior, upstream, columns, other_columns, normed, bundle, back, back_row):
    merged = gather(table, TO_CELLS, {0: block[...], 1: prior[...]})
    pieces = [merged[72 * k : 72 * k + 72] for k in range(4)]
    exact, inverse_std = normalize(jnp.concatenate(pieces, axis=1))
    normed[...] = exact.astype(LOW)
    for k in range(8):
        bundle[k, 0] = columns[k % 2]
        bundle[k, 1] = other_columns[k % 2]
        for half in range(2):
            at = 512 * (k // 2) + 256 * half
            bundle[k, 2 + half] = exact[:, at : at + 256].astype(LOW)
    grads = upstream[...]
    grads = inverse_std * (
        grads
        - jnp.mean(grads, axis=-1, keepdims=True)
        - exact * jnp.mean(grads * exact, axis=-1, keepdims=True)
    )
    stacked = jnp.concatenate([grads[:, 512 * k : 512 * k + 512] for k in range(4)], axis=0)
    stacked = stacked.astype(LOW)
    positions = gather(table, FROM_CELLS, {0: stacked})
    back[...] = positions[:288].astype(LOW)
    back_row[...] = positions[288:].astype(LOW)


def merging_kernel(xh, bundle, other_normed, kept, sent, total):
    for half in range(2):
        terms = 0.0
        for k in range(8):
            terms += dot_tn(bundle[k, 0], bundle[k, 2 + half]) + dot_tn(bundle[k, 1], other_normed[k, half])
        terms = terms.astype(LOW)
        for m in range(16):
            total[32 * m + 16 * half : 32 * m + 16 * half + 16] = terms[16 * m : 16 * m + 16]
    kept[...] = total[pl.ds(pl.multiple_of(256 * xh[0], 256), 256)]
    sent[...] = total[pl.ds(pl.multiple_of(256 - 256 * xh[0], 256), 256)]


def backward_kernel(
    core, table, back, next_row, windows, projected, far_attention, attended, far_inward, outward,
    token_grads, kept, sent, projected_back, inward_t, outward_t, attention, inward, shares_in, weight_in,
):
    loads = [pltpu.make_async_copy(far_attention.at[w], attention.at[w], shares_in.at[w]) for w in range(2)]
    loads.append(pltpu.make_async_copy(far_inward, inward, weight_in))
    for load in loads:
        load.start()
    upstream = gather(table, UPSTREAM, {0: back[...], 1: next_row[...]})
    upstream_low = upstream.astype(LOW)
    attended_back = dot_nt(upstream_low, outward[...]).astype(LOW)
    masks = head_masks()
    for w in range(2):
        rows = slice(144 * w, 144 * w + 144)
        loads[w].wait()
        for t in range(4):
            query = projected[rows, 128 * t : 128 * t + 128]
            key_t = projected[rows, 512 + 128 * t : 640 + 128 * t].T
            value = projected[rows, 1024 + 128 * t : 1152 + 128 * t]
            grads = attended_back[rows, 128 * t : 128 * t + 128]
            query_parts, key_back, value_back = [], 0.0, 0.0
            for h in range(4):
                low = attention[w, 4 * t + h]
                share = low.astype(WIDE)
                product = share * dot_nt(value * masks[h], grads)
                total = jnp.sum(product, axis=0, keepdims=True)
                score_back = ((product - share * total) * SCALE).astype(LOW)
                value_back += dot_nn(low, grads * masks[h])
                key_back += dot_nn(score_back, query * masks[h])
                query_parts.append(dot_nn(key_t[32 * h : 32 * h + 32], score_back))
            query_back = jnp.concatenate(query_parts, axis=0).T
            projected_back[rows, 128 * t : 128 * t + 128] = query_back.astype(LOW)
            projected_back[rows, 512 + 128 * t : 640 + 128 * t] = key_back.astype(LOW)
            projected_back[rows, 1024 + 128 * t : 1152 + 128 * t] = value_back.astype(LOW)
    normed, inverse_std = normalize(windows[...].astype(WIDE))
    normed_low = normed.astype(LOW)
    for j in range(4):
        inward_t[384 * j : 384 * j + 384] = dot_tn(projected_back[:, 384 * j : 384 * j + 384], normed_low).astype(LOW)
    outward_t[...] = dot_tn(upstream_low, attended[...]).astype(LOW)
    mine = core[0]
    for place in range(16):
        for terms, parity in ((kept, mine), (sent, 1 - mine)):
            at = 2 * place + parity
            for k in range(4):
                lanes = slice(128 * k, 128 * k + 128)
                head = pl.ds(pl.multiple_of(48 * at, 16), 32)
                tail = pl.ds(pl.multiple_of(48 * at + 32, 16), 16)
                last = pl.ds(pl.multiple_of(16 * at, 16), 16)
                terms[place // 8, k, 0, place % 8] = inward_t[head, lanes]
                terms[place // 8, k, 1, place % 8, 0:16] = inward_t[tail, lanes]
                terms[place // 8, k, 1, place % 8, 16:32] = outward_t[last, lanes]
    loads[2].wait()
    normed_back = dot_nt(projected_back[...], inward[...])
    branch = inverse_std * (
        normed_back
        - jnp.mean(normed_back, axis=-1, keepdims=True)
        - normed * jnp.mean(normed_back * normed, axis=-1, keepdims=True)
    )
    result = (upstream + branch.astype(LOW).astype(WIDE)).astype(LOW)
    token_grads[...] = gather(table, FROM_WINDOWS, {0: result}).astype(LOW)


def shares_kernel(shares, inward_grads, outward_grads, merging_grads):
    for k in range(4):
        lanes = slice(128 * k, 128 * k + 128)
        inward_grads[0:32, lanes] = shares[2 * k, :, :128].astype(WIDE)
        inward_grads[32:48, lanes] = shares[2 * k + 1, 0:16, :128].astype(WIDE)
        outward_grads[:, lanes] = shares[2 * k + 1, 16:32, :128].astype(WIDE)
        for g in range(2):
            for half in range(2):
                at = 512 * k + 256 * half
                part = shares[2 * k + g, 16 * half : 16 * half + 16, 128:]
                merging_grads[16 * g : 16 * g + 16, at : at + 256] = part.astype(WIDE)


def call(kernel, outs, *operands, scratch=(), scalars=0, room=8, far=(), far_outs=()):
    specs = [pl.BlockSpec()] * len(operands)
    for at in range(scalars):
        specs[at] = pl.BlockSpec(memory_space=pltpu.SMEM)
    for at in far:
        specs[at] = pl.BlockSpec(memory_space=pltpu.HBM)
    out_specs = [pl.BlockSpec(memory_space=pltpu.HBM) if at in far_outs else pl.BlockSpec() for at in range(len(outs))]
    return pl.pallas_call(
        kernel,
        in_specs=specs,
        out_specs=out_specs,
        out_shape=[
            jax.ShapeDtypeStruct(shape[:-1], WIDE) if shape[-1] is WIDE else jax.ShapeDtypeStruct(shape, LOW)
            for shape in outs
        ],
        scratch_shapes=[pltpu.VMEM(shape, LOW) if isinstance(shape, tuple) else shape for shape in scratch],
        compiler_params=pltpu.CompilerParams(vmem_limit_bytes=room * 1024 * 1024),
    )(*operands)


def from_behind(value, axis, steps):
    count = lax.axis_size(axis)
    pairs = [(source, (source + steps) % count) for source in range(count)]
    return lax.ppermute(value, axis, pairs)


def local_windows(layout):
    return layout.reshape(2, 6, 2, 12).transpose(2, 0, 1, 3).reshape(2, 144)


def to_neighbours(parts, steps):
    grp, lat, both = parts
    pairs = [
        (4 * 0 + 2 * row + level, (row + steps) % 4 * 2 + (level + steps) % 2) for row in range(4) for level in range(2)
    ]
    return (
        from_behind(grp, ("grp",), steps),
        from_behind(lat, ("lat",), steps),
        lax.ppermute(both, ("lat", "grp"), pairs),
    )


PLANES = [(120, 512), (96, 512), (96, 512)]


def shift_forward(table, tokens, cells):
    parts = to_neighbours(call(planes_in_kernel, PLANES, table, tokens, cells), -1)
    (columns,) = call(columns_in_kernel, [(108, 512)], table, tokens, cells, *parts)
    return (*parts, from_behind(columns, LON, -1))


def wide_sum(parts):
    return jnp.sum(parts.astype(WIDE), axis=0).astype(LOW)


def over_planes(terms):
    terms = terms.reshape((16,) + terms.shape[3:])
    return wide_sum(lax.all_to_all(terms, ("xh", "lat", "grp"), 0, 0))


def tied(*values):
    return lax.optimization_barrier(values)


def body(fine_tokens, region_ids, inward_weight, outward_weight, merging_weight, coarse_cotangent):
    table = jnp.asarray(TABLE)
    core = lax.axis_index("core").reshape(1)
    tokens = fine_tokens.reshape(288, 512)
    cells = coarse_cotangent.reshape(72, 1024)
    parts = shift_forward(table, tokens, cells)
    labels = local_windows(region_ids)
    block, last_row, windows, projected, attention, attended, shifted, columns, sent_columns = call(
        forward_kernel,
        [
            (288, 512), (48, 512), (288, 512), (288, 1536), (2, HEADS, 144, 144), (288, 512),
            (72, 1024), (2, 72, 256), (2, 72, 256),
        ],
        core, table, tokens, cells, *parts, labels.reshape(2, 1, 144), labels.reshape(2, 144, 1), inward_weight, outward_weight,
        scratch=[
            (512, 1536), (512, 512), (2, HEADS, 144, 144), (1024, 72), (256, 72),
            pltpu.SemaphoreType.DMA((2,)), pltpu.SemaphoreType.DMA((2, 4)),
        ],
        scalars=1, room=54, far=(10, 11), far_outs=(4,),
    )
    prior = from_behind(last_row, ("lat",), 1)
    other_columns = from_behind(sent_columns, ("core",), 1)
    merged_upstream = dot_nt(shifted, merging_weight)
    merged_normed, bundle, back, back_row = call(
        merge_kernel,
        [(72, 2048), (8, 4, 72, 256), (288, 512), (48, 512)],
        table, block, prior, merged_upstream, columns, other_columns,
    )
    next_row = from_behind(back_row, ("lat",), -1)
    next_row, bundle = tied(next_row, bundle)
    bundle = lax.all_to_all(bundle, ("lat", "grp"), 0, 0)
    token_grads, kept, sent = call(
        backward_kernel,
        [(288, 512), (2, 4, 2, 8, 32, 128), (2, 4, 2, 8, 32, 128)],
        core, table, back, next_row, windows, projected, attention, attended, inward_weight, outward_weight,
        scratch=[
            (288, 1536), (1536, 512), (512, 512), (2, HEADS, 144, 144), (512, 1536),
            pltpu.SemaphoreType.DMA((2,)), pltpu.SemaphoreType.DMA,
        ],
        scalars=1, room=54, far=(6, 8),
    )
    merged_normed, token_grads = tied(merged_normed, token_grads)
    coarse_field = dot_nn(merged_normed, merging_weight).astype(LOW)
    kept, sent, bundle, coarse_field = tied(kept, sent, bundle, coarse_field)
    came = from_behind(sent, ("core",), 1)
    block_terms = (kept.astype(WIDE) + came.astype(WIDE)).astype(LOW)
    block_planes = over_planes(block_terms)
    other_normed = from_behind(bundle[:, 2:], ("core",), 1)
    merging_kept, merging_sent = call(
        merging_kernel,
        [(256, 256), (256, 256)],
        lax.axis_index("xh").reshape(1), bundle, other_normed,
        scratch=[(512, 256)], scalars=1,
    )
    merging_came = from_behind(merging_sent, ("xh",), 1)
    (lon_out,) = call(columns_out_kernel, [(108, 512)], table, token_grads, coarse_field)
    lon_out = from_behind(lon_out, LON, 1)
    parts_out = call(planes_out_kernel, PLANES, table, token_grads, coarse_field, lon_out)
    block_planes, merging_came, *parts_out = tied(block_planes, merging_came, *parts_out)
    parts_out = to_neighbours(parts_out, 1)
    merging_planes = (merging_kept.astype(WIDE) + merging_came.astype(WIDE)).astype(LOW).reshape(8, 32, 256)
    planes = jnp.concatenate([block_planes, merging_planes], axis=2)
    share = wide_sum(lax.all_to_all(planes, ("z",), 0, 0))
    share, *parts_out = tied(share, *parts_out)
    shares = lax.all_to_all(jnp.broadcast_to(share[None], (8, 32, 384)), ("lat", "grp"), 0, 0)
    token_grads, coarse_field = call(
        all_out_kernel, [(288, 512), (72, 1024)], table, token_grads, coarse_field, *parts_out, lon_out
    )
    grads = call(shares_kernel, [(48, 512, WIDE), (16, 512, WIDE), (32, 2048, WIDE)], shares)
    return (
        coarse_field.reshape(2, 3, 12, 1024),
        token_grads.reshape(2, 6, 24, 512),
        *(share.T for share in grads),
    )


def solution(mesh):
    fine = Mesh(mesh.devices.reshape(4, 2, 8, 2, 2), ("lat", "xh", "z", "core", "grp"))
    return jax.shard_map(
        body,
        mesh=fine,
        in_specs=(
            P("grp", "lat", LON, None),
            P("grp", "lat", LON),
            P(),
            P(),
            P(),
            P("grp", "lat", LON, None),
        ),
        out_specs=(
            P("grp", "lat", LON, None),
            P("grp", "lat", LON, None),
            P(None, LON),
            P(None, LON),
            P(None, LON),
        ),
        check_vma=False,
    )
```

```python
import jax
import jax.numpy as jnp
import numpy as np
from jax import lax
from jax.experimental import pallas as pl
from jax.experimental.pallas import tpu as pltpu
from jax.sharding import Mesh, PartitionSpec as P

HEADS = 16
LON = ("xh", "z", "core")
SCALE = 32 ** (-0.5)
LOW = jnp.bfloat16
WIDE = jnp.float32


def halves(fields):
    return np.concatenate([fields.reshape(-1), (fields + 1000).reshape(-1)])


def join(*parts):
    return np.concatenate([part.reshape(-1) for part in parts])


FINE_AT = np.arange(288).reshape(2, 6, 24)
CELL_AT = 1000 + np.arange(72).reshape(2, 3, 12)


def arrived(source, rows):
    fine = 1000 * source + np.arange(72).reshape(3, 24)
    cells = 1000 * source + 72 + np.arange(12 * rows).reshape(rows, 12)
    return fine, cells, 12 * rows


def shift_in():
    grp, lat, both = arrived(3, 2), arrived(4, 1), arrived(5, 1)
    first = [
        join(FINE_AT[0, 3:], halves(CELL_AT[0, 1:])),
        join(FINE_AT[1, :3], halves(CELL_AT[1, :1])),
        join(FINE_AT[0, :3], halves(CELL_AT[0, :1])),
    ]
    fine = np.stack([np.concatenate([FINE_AT[1, 3:], lat[0]]), np.concatenate([grp[0], both[0]])])
    left = np.stack([np.concatenate([CELL_AT[1, 1:], lat[1]]), np.concatenate([grp[1], both[1]])])
    right = np.stack(
        [np.concatenate([CELL_AT[1, 1:] + 1000, lat[1] + lat[2]]), np.concatenate([grp[1] + grp[2], both[1] + both[2]])]
    )
    second = join(fine[:, :, :6], left[:, :, :3], right[:, :, :3])
    lon_fine = 6000 + np.arange(72).reshape(2, 6, 6)
    lon_cells = 6072 + np.arange(18).reshape(2, 3, 3)
    fine = np.concatenate([fine[:, :, 6:], lon_fine], axis=2)
    left = np.concatenate([left[:, :, 3:], lon_cells], axis=2)
    right = np.concatenate([right[:, :, 3:], lon_cells + 18], axis=2)
    windows = fine.reshape(2, 6, 2, 12).transpose(2, 0, 1, 3)
    return join(*first), second, windows.reshape(-1), join(left, right)


def shift_out():
    first = join(FINE_AT[:, :, 18:], CELL_AT[:, :, 9:], CELL_AT[:, :, 9:] + 1000)
    lon_fine = 6000 + np.arange(72).reshape(2, 6, 6)
    lon_cells = 6072 + np.arange(18).reshape(2, 3, 3)
    fine = np.concatenate([lon_fine, FINE_AT[:, :, :18]], axis=2)
    left = np.concatenate([lon_cells, CELL_AT[:, :, :9]], axis=2)
    right = np.concatenate([lon_cells + 18, CELL_AT[:, :, :9] + 1000], axis=2)
    second = join(
        fine[1, :3], left[1, :2], right[1, :2], fine[0, 3:], left[0, 2], right[0, 2], fine[1, 3:], left[1, 2], right[1, 2]
    )
    grp, lat, both = arrived(3, 2), arrived(4, 1), arrived(5, 1)
    fine = np.stack([np.concatenate([both[0], grp[0]]), np.concatenate([lat[0], fine[0, :3]])])
    left = np.stack([np.concatenate([both[1], grp[1]]), np.concatenate([lat[1], left[0, :2]])])
    right = np.stack(
        [np.concatenate([both[1] + both[2], grp[1] + grp[2]]), np.concatenate([lat[1] + lat[2], right[0, :2]])]
    )
    return first, second, join(fine, left, right)


def block_maps():
    natural = np.arange(288).reshape(2, 6, 24)
    windows = natural.reshape(2, 6, 2, 12).transpose(2, 0, 1, 3).reshape(288)
    extended = np.concatenate([1000 + np.arange(48).reshape(2, 1, 24), natural[:, :5]], axis=1)
    to_cells = extended.reshape(2, 3, 2, 12, 2).transpose(4, 2, 0, 1, 3).reshape(288)
    from_cells = np.full(336, -1)
    from_cells[np.where(to_cells < 1000, to_cells, to_cells - 712)] = np.arange(288)
    replaced = natural.copy()
    replaced[:, 5] = 1000 + np.arange(48).reshape(2, 24)
    return np.argsort(windows), to_cells, from_cells, replaced.reshape(288)[windows]


def row_table():
    columns = [*shift_in(), *shift_out(), *block_maps()]
    table = np.full((432, len(columns)), -1, np.int32)
    for at, column in enumerate(columns):
        table[: len(column), at] = column
    return table


TABLE = row_table()
(
    IN_FIRST, IN_SECOND, IN_WINDOWS, IN_CELLS, OUT_FIRST, OUT_SECOND, OUT_ALL,
    FROM_WINDOWS, TO_CELLS, FROM_CELLS, UPSTREAM,
) = range(11)
ROWS = [int((TABLE[:, at] >= 0).sum()) for at in range(11)]
ROWS[FROM_CELLS] = 336


def gather(table, column, sources):
    return gather_named(table[: ROWS[column], column : column + 1], sources)


def gather_named(names, sources):
    total = 0.0
    for source, value in sources.items():
        place = lax.broadcasted_iota(jnp.int32, (names.shape[0], value.shape[0]), 1) + 1000 * source
        total += dot_nn((names == place).astype(WIDE).astype(LOW), value)
    return total


def dot_nn(a, b):
    return lax.dot_general(a, b, (((1,), (0,)), ((), ())), preferred_element_type=WIDE)


def dot_nt(a, b):
    return lax.dot_general(a, b, (((1,), (1,)), ((), ())), preferred_element_type=WIDE)


def dot_tn(a, b):
    return lax.dot_general(a, b, (((0,), (0,)), ((), ())), preferred_element_type=WIDE)


def head_masks():
    head = lax.broadcasted_iota(jnp.int32, (144, 128), 1) >> 5
    return [(head == h).astype(WIDE).astype(LOW) for h in range(4)]


def normalize(values):
    centred = values - jnp.mean(values, axis=-1, keepdims=True)
    inverse_std = lax.rsqrt(jnp.mean(centred * centred, axis=-1, keepdims=True) + 1e-05)
    return (centred * inverse_std, inverse_std)


def own(tokens, cells):
    return {0: tokens[...], 1: cells[:, :512], 2: cells[:, 512:]}


def arrivals(grp, lat, both):
    return {3: grp[...], 4: lat[...], 5: both[...]}


def store_planes(packed, grp, lat, both):
    grp[...] = packed[:120].astype(LOW)
    lat[...] = packed[120:216].astype(LOW)
    both[...] = packed[216:].astype(LOW)


def runs(target):
    target = np.asarray(target)
    begins = [0] + [at for at in range(1, len(target)) if target[at] != target[at - 1] + 1]
    return [(at, int(target[at]) - at) for at in begins]


def planes_in_kernel(tokens, cells, *outs):
    row = lax.broadcasted_iota(jnp.int32, (ROWS[IN_FIRST], 1), 0)
    ahead = jnp.zeros_like(row)
    for begin, difference in runs(TABLE[: ROWS[IN_FIRST], IN_FIRST]):
        ahead = jnp.where(row >= begin, difference, ahead)
    store_planes(gather_named(row + ahead, own(tokens, cells)), *outs)


def columns_in_kernel(table, tokens, cells, grp, lat, both, out):
    out[...] = gather(table, IN_SECOND, own(tokens, cells) | arrivals(grp, lat, both)).astype(LOW)


def columns_out_kernel(table, tokens, cells, out):
    out[...] = gather(table, OUT_FIRST, own(tokens, cells)).astype(LOW)


def planes_out_kernel(table, tokens, cells, lon, *outs):
    store_planes(gather(table, OUT_SECOND, own(tokens, cells) | {6: lon[...]}), *outs)


def all_out_kernel(table, tokens, cells, grp, lat, both, lon, fine, coarse):
    packed = gather(table, OUT_ALL, own(tokens, cells) | arrivals(grp, lat, both) | {6: lon[...]})
    fine[...] = packed[:288].astype(LOW)
    coarse[:, :512] = packed[288:360].astype(LOW)
    coarse[:, 512:] = packed[360:].astype(LOW)


def shift_cotangent(core, table, sources, shifted, kept, sent, columns, picked):
    packed = gather(table, IN_CELLS, sources)
    cotangent = jnp.concatenate([packed[:72], packed[72:]], axis=1)
    shifted[...] = cotangent.astype(LOW)
    columns[...] = cotangent.T.astype(LOW)
    for out, parity in ((kept, core[0]), (sent, 1 - core[0])):
        for g in range(2):
            for m in range(16):
                at = pl.multiple_of(64 * m + 32 * parity + 16 * g, 16)
                picked[16 * m : 16 * m + 16] = columns[pl.ds(at, 16)]
            out[g] = picked[...].astype(WIDE).T.astype(LOW)


def forward_kernel(
    core, table, tokens, cells, grp, lat, both, lon, row_labels, column_labels, far_inward, far_outward,
    block, last_row, far_windows, far_projected, far_attention, attended, shifted, kept, sent,
    inward, outward, attention, columns, picked, windows, projected, weights_in, shares_out, early_out,
):
    fetches = [
        pltpu.make_async_copy(far_inward, inward, weights_in.at[0]),
        pltpu.make_async_copy(far_outward, outward, weights_in.at[1]),
    ]
    for copy in fetches:
        copy.start()
    stores = [
        pltpu.make_async_copy(windows, far_windows, early_out.at[0]),
        pltpu.make_async_copy(projected, far_projected, early_out.at[1]),
    ]
    arrived_parts = arrivals(grp, lat, both) | {6: lon[...]}
    values = gather(table, IN_WINDOWS, {0: tokens[...]} | arrived_parts)
    windows[...] = values.astype(LOW)
    stores[0].start()
    normed = normalize(values)[0].astype(LOW)
    fetches[0].wait()
    projected[...] = dot_nn(normed, inward[...]).astype(LOW)
    stores[1].start()
    masks = head_masks()
    for w in range(2):
        rows = slice(144 * w, 144 * w + 144)
        allowed = column_labels[w] == row_labels[w]
        for t in range(4):
            query = projected[rows, 128 * t : 128 * t + 128]
            key = projected[rows, 512 + 128 * t : 640 + 128 * t]
            value_t = projected[rows, 1024 + 128 * t : 1152 + 128 * t].T
            parts = []
            for h in range(4):
                scores = dot_nt(key * masks[h], query) * SCALE
                scores = jnp.where(allowed, scores, -1e30)
                weights = jnp.exp(scores - jnp.max(scores, axis=0, keepdims=True))
                share = weights * (1.0 / jnp.sum(weights, axis=0, keepdims=True))
                share = share.astype(LOW)
                attention[w, 4 * t + h] = share
                parts.append(dot_nn(value_t[32 * h : 32 * h + 32], share))
            attended[rows, 128 * t : 128 * t + 128] = jnp.concatenate(parts, axis=0).T.astype(LOW)
            heads = pl.ds(4 * t, 4)
            store = pltpu.make_async_copy(attention.at[w, heads], far_attention.at[w, heads], shares_out.at[w, t])
            store.start()
            stores.append(store)
    fetches[1].wait()
    result = (values + dot_nn(attended[...], outward[...])).astype(LOW)
    natural = gather(table, FROM_WINDOWS, {0: result})
    block[...] = natural.astype(LOW)
    last_row[...] = jnp.concatenate([natural[120:144], natural[264:]], axis=0).astype(LOW)
    cell_parts = {1: cells[:, :512], 2: cells[:, 512:]} | arrived_parts
    shift_cotangent(core, table, cell_parts, shifted, kept, sent, columns, picked)
    for store in stores:
        store.wait()


def merge_kernel(table, block, prior, upstream, columns, other_columns, normed, bundle, far_back, back_row, back, back_out):
    merged = gather(table, TO_CELLS, {0: block[...], 1: prior[...]})
    pieces = [merged[72 * k : 72 * k + 72] for k in range(4)]
    exact, inverse_std = normalize(jnp.concatenate(pieces, axis=1))
    grads = upstream[...]
    grads = inverse_std * (
        grads
        - jnp.mean(grads, axis=-1, keepdims=True)
        - exact * jnp.mean(grads * exact, axis=-1, keepdims=True)
    )
    stacked = jnp.concatenate([grads[:, 512 * k : 512 * k + 512] for k in range(4)], axis=0)
    stacked = stacked.astype(LOW)
    positions = gather(table, FROM_CELLS, {0: stacked})
    back[...] = positions[:288].astype(LOW)
    store = pltpu.make_async_copy(back, far_back, back_out)
    store.start()
    back_row[...] = positions[288:].astype(LOW)
    normed[...] = exact.astype(LOW)
    for k in range(8):
        bundle[k, 0] = columns[k % 2]
        bundle[k, 1] = other_columns[k % 2]
        for half in range(2):
            at = 512 * (k // 2) + 256 * half
            bundle[k, 2 + half] = exact[:, at : at + 256].astype(LOW)
    store.wait()


def merging_kernel(xh, bundle, other_normed, kept, sent, total):
    for half in range(2):
        terms = 0.0
        for k in range(8):
            terms += dot_tn(bundle[k, 0], bundle[k, 2 + half]) + dot_tn(bundle[k, 1], other_normed[k, half])
        terms = terms.astype(LOW)
        for m in range(16):
            total[32 * m + 16 * half : 32 * m + 16 * half + 16] = terms[16 * m : 16 * m + 16]
    kept[...] = total[pl.ds(pl.multiple_of(256 * xh[0], 256), 256)]
    sent[...] = total[pl.ds(pl.multiple_of(256 - 256 * xh[0], 256), 256)]


def backward_kernel(
    core, table, back, next_row, windows, projected, far_attention, attended, far_inward, outward,
    token_grads, far_kept, far_sent,
    projected_back, inward_t, outward_t, attention, inward, kept, sent, shares_in, weight_in, terms_out,
):
    loads = [pltpu.make_async_copy(far_attention.at[w], attention.at[w], shares_in.at[w]) for w in range(2)]
    loads.append(pltpu.make_async_copy(far_inward, inward, weight_in))
    for load in loads:
        load.start()
    upstream = gather(table, UPSTREAM, {0: back[...], 1: next_row[...]})
    upstream_low = upstream.astype(LOW)
    attended_back = dot_nt(upstream_low, outward[...]).astype(LOW)
    masks = head_masks()
    for w in range(2):
        rows = slice(144 * w, 144 * w + 144)
        loads[w].wait()
        for t in range(4):
            query = projected[rows, 128 * t : 128 * t + 128]
            key_t = projected[rows, 512 + 128 * t : 640 + 128 * t].T
            value = projected[rows, 1024 + 128 * t : 1152 + 128 * t]
            grads = attended_back[rows, 128 * t : 128 * t + 128]
            query_parts, key_back, value_back = [], 0.0, 0.0
            for h in range(4):
                low = attention[w, 4 * t + h]
                share = low.astype(WIDE)
                product = share * dot_nt(value * masks[h], grads)
                total = jnp.sum(product, axis=0, keepdims=True)
                score_back = ((product - share * total) * SCALE).astype(LOW)
                value_back += dot_nn(low, grads * masks[h])
                key_back += dot_nn(score_back, query * masks[h])
                query_parts.append(dot_nn(key_t[32 * h : 32 * h + 32], score_back))
            query_back = jnp.concatenate(query_parts, axis=0).T
            projected_back[rows, 128 * t : 128 * t + 128] = query_back.astype(LOW)
            projected_back[rows, 512 + 128 * t : 640 + 128 * t] = key_back.astype(LOW)
            projected_back[rows, 1024 + 128 * t : 1152 + 128 * t] = value_back.astype(LOW)
    normed, inverse_std = normalize(windows[...].astype(WIDE))
    normed_low = normed.astype(LOW)
    for j in range(4):
        inward_t[384 * j : 384 * j + 384] = dot_tn(projected_back[:, 384 * j : 384 * j + 384], normed_low).astype(LOW)
    outward_t[...] = dot_tn(upstream_low, attended[...]).astype(LOW)
    mine = core[0]
    for place in range(16):
        for terms, parity in ((kept, mine), (sent, 1 - mine)):
            at = 2 * place + parity
            for k in range(4):
                lanes = slice(128 * k, 128 * k + 128)
                head = pl.ds(pl.multiple_of(48 * at, 16), 32)
                tail = pl.ds(pl.multiple_of(48 * at + 32, 16), 16)
                last = pl.ds(pl.multiple_of(16 * at, 16), 16)
                terms[place // 8, k, 0, place % 8] = inward_t[head, lanes]
                terms[place // 8, k, 1, place % 8, 0:16] = inward_t[tail, lanes]
                terms[place // 8, k, 1, place % 8, 16:32] = outward_t[last, lanes]
    stores = [
        pltpu.make_async_copy(sent, far_sent, terms_out.at[0]),
        pltpu.make_async_copy(kept, far_kept, terms_out.at[1]),
    ]
    for store in stores:
        store.start()
    loads[2].wait()
    normed_back = dot_nt(projected_back[...], inward[...])
    branch = inverse_std * (
        normed_back
        - jnp.mean(normed_back, axis=-1, keepdims=True)
        - normed * jnp.mean(normed_back * normed, axis=-1, keepdims=True)
    )
    result = (upstream + branch.astype(LOW).astype(WIDE)).astype(LOW)
    token_grads[...] = gather(table, FROM_WINDOWS, {0: result}).astype(LOW)
    for store in stores:
        store.wait()


def shares_kernel(shares, inward_grads, outward_grads, merging_grads):
    for k in range(4):
        lanes = slice(128 * k, 128 * k + 128)
        inward_grads[0:32, lanes] = shares[2 * k, :, :128].astype(WIDE)
        inward_grads[32:48, lanes] = shares[2 * k + 1, 0:16, :128].astype(WIDE)
        outward_grads[:, lanes] = shares[2 * k + 1, 16:32, :128].astype(WIDE)
        for g in range(2):
            for half in range(2):
                at = 512 * k + 256 * half
                part = shares[2 * k + g, 16 * half : 16 * half + 16, 128:]
                merging_grads[16 * g : 16 * g + 16, at : at + 256] = part.astype(WIDE)


def call(kernel, outs, *operands, scratch=(), scalars=0, room=8, far=(), far_outs=()):
    specs = [pl.BlockSpec()] * len(operands)
    for at in range(scalars):
        specs[at] = pl.BlockSpec(memory_space=pltpu.SMEM)
    for at in far:
        specs[at] = pl.BlockSpec(memory_space=pltpu.HBM)
    out_specs = [pl.BlockSpec(memory_space=pltpu.HBM) if at in far_outs else pl.BlockSpec() for at in range(len(outs))]
    return pl.pallas_call(
        kernel,
        in_specs=specs,
        out_specs=out_specs,
        out_shape=[
            jax.ShapeDtypeStruct(shape[:-1], WIDE) if shape[-1] is WIDE else jax.ShapeDtypeStruct(shape, LOW)
            for shape in outs
        ],
        scratch_shapes=[pltpu.VMEM(shape, LOW) if isinstance(shape, tuple) else shape for shape in scratch],
        compiler_params=pltpu.CompilerParams(vmem_limit_bytes=room * 1024 * 1024),
    )(*operands)


def from_behind(value, axis, steps):
    count = lax.axis_size(axis)
    pairs = [(source, (source + steps) % count) for source in range(count)]
    return lax.ppermute(value, axis, pairs)


def local_windows(layout):
    return layout.reshape(2, 6, 2, 12).transpose(2, 0, 1, 3).reshape(2, 144)


def to_neighbours(parts, steps):
    grp, lat, both = parts
    pairs = [
        (4 * 0 + 2 * row + level, (row + steps) % 4 * 2 + (level + steps) % 2) for row in range(4) for level in range(2)
    ]
    return (
        from_behind(grp, ("grp",), steps),
        from_behind(lat, ("lat",), steps),
        lax.ppermute(both, ("lat", "grp"), pairs),
    )


PLANES = [(120, 512), (96, 512), (96, 512)]


def shift_forward(table, tokens, cells):
    parts = to_neighbours(call(planes_in_kernel, PLANES, tokens, cells), -1)
    (columns,) = call(columns_in_kernel, [(108, 512)], table, tokens, cells, *parts)
    return (*parts, from_behind(columns, LON, -1))


def wide_sum(parts):
    return jnp.sum(parts.astype(WIDE), axis=0).astype(LOW)


def over_planes(terms):
    terms = terms.reshape((16,) + terms.shape[3:])
    return wide_sum(lax.all_to_all(terms, ("xh", "lat", "grp"), 0, 0))


def tied(*values):
    return lax.optimization_barrier(values)


def body(fine_tokens, region_ids, inward_weight, outward_weight, merging_weight, coarse_cotangent):
    table = jnp.asarray(TABLE)
    core = lax.axis_index("core").reshape(1)
    tokens = fine_tokens.reshape(288, 512)
    cells = coarse_cotangent.reshape(72, 1024)
    parts = shift_forward(table, tokens, cells)
    labels = local_windows(region_ids)
    block, last_row, windows, projected, attention, attended, shifted, columns, sent_columns = call(
        forward_kernel,
        [
            (288, 512), (48, 512), (288, 512), (288, 1536), (2, HEADS, 144, 144), (288, 512),
            (72, 1024), (2, 72, 256), (2, 72, 256),
        ],
        core, table, tokens, cells, *parts, labels.reshape(2, 1, 144), labels.reshape(2, 144, 1), inward_weight, outward_weight,
        scratch=[
            (512, 1536), (512, 512), (2, HEADS, 144, 144), (1024, 72), (256, 72), (288, 512), (288, 1536),
            pltpu.SemaphoreType.DMA((2,)), pltpu.SemaphoreType.DMA((2, 4)), pltpu.SemaphoreType.DMA((2,)),
        ],
        scalars=1, room=54, far=(10, 11), far_outs=(2, 3, 4),
    )
    prior = from_behind(last_row, ("lat",), 1)
    other_columns = from_behind(sent_columns, ("core",), 1)
    merged_upstream = dot_nt(shifted, merging_weight)
    merged_normed, bundle, back, back_row = call(
        merge_kernel,
        [(72, 2048), (8, 4, 72, 256), (288, 512), (48, 512)],
        table, block, prior, merged_upstream, columns, other_columns,
        scratch=[(288, 512), pltpu.SemaphoreType.DMA], far_outs=(2,),
    )
    next_row = from_behind(back_row, ("lat",), -1)
    next_row, bundle = tied(next_row, bundle)
    bundle = lax.all_to_all(bundle, ("lat", "grp"), 0, 0)
    token_grads, kept, sent = call(
        backward_kernel,
        [(288, 512), (2, 4, 2, 8, 32, 128), (2, 4, 2, 8, 32, 128)],
        core, table, back, next_row, windows, projected, attention, attended, inward_weight, outward_weight,
        scratch=[
            (288, 1536), (1536, 512), (512, 512), (2, HEADS, 144, 144), (512, 1536),
            (2, 4, 2, 8, 32, 128), (2, 4, 2, 8, 32, 128),
            pltpu.SemaphoreType.DMA((2,)), pltpu.SemaphoreType.DMA, pltpu.SemaphoreType.DMA((2,)),
        ],
        scalars=1, room=54, far=(6, 8), far_outs=(1, 2),
    )
    merged_normed, token_grads = tied(merged_normed, token_grads)
    coarse_field = dot_nn(merged_normed, merging_weight).astype(LOW)
    kept, sent, bundle, coarse_field = tied(kept, sent, bundle, coarse_field)
    came = from_behind(sent, ("core",), 1)
    block_terms = (kept.astype(WIDE) + came.astype(WIDE)).astype(LOW)
    block_planes = over_planes(block_terms)
    other_normed = from_behind(bundle[:, 2:], ("core",), 1)
    merging_kept, merging_sent = call(
        merging_kernel,
        [(256, 256), (256, 256)],
        lax.axis_index("xh").reshape(1), bundle, other_normed,
        scratch=[(512, 256)], scalars=1,
    )
    merging_came = from_behind(merging_sent, ("xh",), 1)
    (lon_out,) = call(columns_out_kernel, [(108, 512)], table, token_grads, coarse_field)
    lon_out = from_behind(lon_out, LON, 1)
    parts_out = call(planes_out_kernel, PLANES, table, token_grads, coarse_field, lon_out)
    block_planes, merging_came, *parts_out = tied(block_planes, merging_came, *parts_out)
    parts_out = to_neighbours(parts_out, 1)
    merging_planes = (merging_kept.astype(WIDE) + merging_came.astype(WIDE)).astype(LOW).reshape(8, 32, 256)
    planes = jnp.concatenate([block_planes, merging_planes], axis=2)
    share = wide_sum(lax.all_to_all(planes, ("z",), 0, 0))
    share, first = tied(share, parts_out[0])
    parts_out = (first, *parts_out[1:])
    shares = lax.all_to_all(jnp.broadcast_to(share[None], (8, 32, 384)), ("lat", "grp"), 0, 0)
    token_grads, coarse_field = call(
        all_out_kernel, [(288, 512), (72, 1024)], table, token_grads, coarse_field, *parts_out, lon_out
    )
    grads = call(shares_kernel, [(48, 512, WIDE), (16, 512, WIDE), (32, 2048, WIDE)], shares)
    return (
        coarse_field.reshape(2, 3, 12, 1024),
        token_grads.reshape(2, 6, 24, 512),
        *(share.T for share in grads),
    )


def solution(mesh):
    fine = Mesh(mesh.devices.reshape(4, 2, 8, 2, 2), ("lat", "xh", "z", "core", "grp"))
    return jax.shard_map(
        body,
        mesh=fine,
        in_specs=(
            P("grp", "lat", LON, None),
            P("grp", "lat", LON),
            P(),
            P(),
            P(),
            P("grp", "lat", LON, None),
        ),
        out_specs=(
            P("grp", "lat", LON, None),
            P("grp", "lat", LON, None),
            P(None, LON),
            P(None, LON),
            P(None, LON),
        ),
        check_vma=False,
    )
```

```python
import jax
import jax.numpy as jnp
import numpy as np
from jax import lax
from jax.experimental import pallas as pl
from jax.experimental.pallas import tpu as pltpu
from jax.sharding import Mesh, PartitionSpec as P

HEADS = 16
LON = ("xh", "z", "core")
SCALE = 32 ** (-0.5)
LOW = jnp.bfloat16
WIDE = jnp.float32


def halves(fields):
    return np.concatenate([fields.reshape(-1), (fields + 1000).reshape(-1)])


def join(*parts):
    return np.concatenate([part.reshape(-1) for part in parts])


FINE_AT = np.arange(288).reshape(2, 6, 24)
CELL_AT = 1000 + np.arange(72).reshape(2, 3, 12)


def arrived(source, rows):
    fine = 1000 * source + np.arange(72).reshape(3, 24)
    cells = 1000 * source + 72 + np.arange(12 * rows).reshape(rows, 12)
    return fine, cells, 12 * rows


def shift_in():
    grp, lat, both = arrived(3, 2), arrived(4, 1), arrived(5, 1)
    first = [
        join(FINE_AT[0, 3:], halves(CELL_AT[0, 1:])),
        join(FINE_AT[1, :3], halves(CELL_AT[1, :1])),
        join(FINE_AT[0, :3], halves(CELL_AT[0, :1])),
    ]
    fine = np.stack([np.concatenate([FINE_AT[1, 3:], lat[0]]), np.concatenate([grp[0], both[0]])])
    left = np.stack([np.concatenate([CELL_AT[1, 1:], lat[1]]), np.concatenate([grp[1], both[1]])])
    right = np.stack(
        [np.concatenate([CELL_AT[1, 1:] + 1000, lat[1] + lat[2]]), np.concatenate([grp[1] + grp[2], both[1] + both[2]])]
    )
    second = join(fine[:, :, :6], left[:, :, :3], right[:, :, :3])
    lon_fine = 6000 + np.arange(72).reshape(2, 6, 6)
    lon_cells = 6072 + np.arange(18).reshape(2, 3, 3)
    fine = np.concatenate([fine[:, :, 6:], lon_fine], axis=2)
    left = np.concatenate([left[:, :, 3:], lon_cells], axis=2)
    right = np.concatenate([right[:, :, 3:], lon_cells + 18], axis=2)
    windows = fine.reshape(2, 6, 2, 12).transpose(2, 0, 1, 3)
    return join(*first), second, windows.reshape(-1), join(left, right)


def shift_out():
    first = join(
        FINE_AT[1, :3], halves(CELL_AT[1, :2]), FINE_AT[0, 3:], halves(CELL_AT[0, 2:]), FINE_AT[1, 3:], halves(CELL_AT[1, 2:])
    )
    grp, lat, both = arrived(3, 2), arrived(4, 1), arrived(5, 1)
    fine = np.stack([np.concatenate([both[0], grp[0]]), np.concatenate([lat[0], FINE_AT[0, :3]])])
    left = np.stack([np.concatenate([both[1], grp[1]]), np.concatenate([lat[1], CELL_AT[0, :2]])])
    right = np.stack(
        [
            np.concatenate([both[1] + both[2], grp[1] + grp[2]]),
            np.concatenate([lat[1] + lat[2], CELL_AT[0, :2] + 1000]),
        ]
    )
    second = join(fine[:, :, 18:], left[:, :, 9:], right[:, :, 9:])
    lon_fine = 6000 + np.arange(72).reshape(2, 6, 6)
    lon_cells = 6072 + np.arange(18).reshape(2, 3, 3)
    fine = np.concatenate([lon_fine, fine[:, :, :18]], axis=2)
    left = np.concatenate([lon_cells, left[:, :, :9]], axis=2)
    right = np.concatenate([lon_cells + 18, right[:, :, :9]], axis=2)
    return first, second, join(fine, left, right)


def block_maps():
    natural = np.arange(288).reshape(2, 6, 24)
    windows = natural.reshape(2, 6, 2, 12).transpose(2, 0, 1, 3).reshape(288)
    extended = np.concatenate([1000 + np.arange(48).reshape(2, 1, 24), natural[:, :5]], axis=1)
    to_cells = extended.reshape(2, 3, 2, 12, 2).transpose(4, 2, 0, 1, 3).reshape(288)
    from_cells = np.full(336, -1)
    from_cells[np.where(to_cells < 1000, to_cells, to_cells - 712)] = np.arange(288)
    replaced = natural.copy()
    replaced[:, 5] = 1000 + np.arange(48).reshape(2, 24)
    return np.argsort(windows), to_cells, from_cells, replaced.reshape(288)[windows]


def row_table():
    columns = [*shift_in(), *shift_out(), *block_maps()]
    table = np.full((432, len(columns)), -1, np.int32)
    for at, column in enumerate(columns):
        table[: len(column), at] = column
    return table


TABLE = row_table()
(
    IN_FIRST, IN_SECOND, IN_WINDOWS, IN_CELLS, OUT_FIRST, OUT_SECOND, OUT_ALL,
    FROM_WINDOWS, TO_CELLS, FROM_CELLS, UPSTREAM,
) = range(11)
ROWS = [int((TABLE[:, at] >= 0).sum()) for at in range(11)]
ROWS[FROM_CELLS] = 336


def gather(table, column, sources):
    return gather_named(table[: ROWS[column], column : column + 1], sources)


def gather_named(names, sources):
    total = 0.0
    for source, value in sources.items():
        place = lax.broadcasted_iota(jnp.int32, (names.shape[0], value.shape[0]), 1) + 1000 * source
        total += dot_nn((names == place).astype(WIDE).astype(LOW), value)
    return total


def dot_nn(a, b):
    return lax.dot_general(a, b, (((1,), (0,)), ((), ())), preferred_element_type=WIDE)


def dot_nt(a, b):
    return lax.dot_general(a, b, (((1,), (1,)), ((), ())), preferred_element_type=WIDE)


def dot_tn(a, b):
    return lax.dot_general(a, b, (((0,), (0,)), ((), ())), preferred_element_type=WIDE)


def head_masks():
    head = lax.broadcasted_iota(jnp.int32, (144, 128), 1) >> 5
    return [(head == h).astype(WIDE).astype(LOW) for h in range(4)]


def normalize(values):
    centred = values - jnp.mean(values, axis=-1, keepdims=True)
    inverse_std = lax.rsqrt(jnp.mean(centred * centred, axis=-1, keepdims=True) + 1e-05)
    return (centred * inverse_std, inverse_std)


def own(tokens, cells):
    return {0: tokens[...], 1: cells[:, :512], 2: cells[:, 512:]}


def arrivals(grp, lat, both):
    return {3: grp[...], 4: lat[...], 5: both[...]}


def store_planes(packed, grp, lat, both):
    grp[...] = packed[:120].astype(LOW)
    lat[...] = packed[120:216].astype(LOW)
    both[...] = packed[216:].astype(LOW)


def runs(target):
    target = np.asarray(target)
    begins = [0] + [at for at in range(1, len(target)) if target[at] != target[at - 1] + 1]
    return [(at, int(target[at]) - at) for at in begins]


def column_names(column):
    row = lax.broadcasted_iota(jnp.int32, (ROWS[column], 1), 0)
    ahead = jnp.zeros_like(row)
    for begin, difference in runs(TABLE[: ROWS[column], column]):
        ahead = jnp.where(row >= begin, difference, ahead)
    return row + ahead


def planes_in_kernel(tokens, cells, *outs):
    store_planes(gather_named(column_names(IN_FIRST), own(tokens, cells)), *outs)


def columns_in_kernel(tokens, cells, grp, lat, both, out):
    sources = own(tokens, cells) | arrivals(grp, lat, both)
    out[...] = gather_named(column_names(IN_SECOND), sources).astype(LOW)


def planes_out_kernel(table, tokens, cells, *outs):
    store_planes(gather(table, OUT_FIRST, own(tokens, cells)), *outs)


def columns_out_kernel(table, tokens, cells, grp, lat, both, out):
    out[...] = gather(table, OUT_SECOND, own(tokens, cells) | arrivals(grp, lat, both)).astype(LOW)


def all_out_kernel(table, tokens, cells, grp, lat, both, lon, fine, coarse):
    packed = gather(table, OUT_ALL, own(tokens, cells) | arrivals(grp, lat, both) | {6: lon[...]})
    fine[...] = packed[:288].astype(LOW)
    coarse[:, :512] = packed[288:360].astype(LOW)
    coarse[:, 512:] = packed[360:].astype(LOW)


def shift_cotangent(core, table, sources, shifted, kept, sent, columns, picked):
    packed = gather(table, IN_CELLS, sources)
    cotangent = jnp.concatenate([packed[:72], packed[72:]], axis=1)
    shifted[...] = cotangent.astype(LOW)
    columns[...] = cotangent.T.astype(LOW)
    for out, parity in ((kept, core[0]), (sent, 1 - core[0])):
        for g in range(2):
            for m in range(16):
                at = pl.multiple_of(64 * m + 32 * parity + 16 * g, 16)
                picked[16 * m : 16 * m + 16] = columns[pl.ds(at, 16)]
            out[g] = picked[...].astype(WIDE).T.astype(LOW)


def forward_kernel(
    core, table, tokens, cells, grp, lat, both, lon, row_labels, column_labels, far_inward, far_outward,
    block, last_row, far_windows, far_projected, far_attention, attended, shifted, kept, sent,
    inward, outward, attention, columns, picked, windows, projected, weights_in, shares_out, early_out,
):
    fetches = [
        pltpu.make_async_copy(far_inward, inward, weights_in.at[0]),
        pltpu.make_async_copy(far_outward, outward, weights_in.at[1]),
    ]
    for copy in fetches:
        copy.start()
    stores = [
        pltpu.make_async_copy(windows, far_windows, early_out.at[0]),
        pltpu.make_async_copy(projected, far_projected, early_out.at[1]),
    ]
    arrived_parts = arrivals(grp, lat, both) | {6: lon[...]}
    values = gather(table, IN_WINDOWS, {0: tokens[...]} | arrived_parts)
    windows[...] = values.astype(LOW)
    stores[0].start()
    normed = normalize(values)[0].astype(LOW)
    fetches[0].wait()
    projected[...] = dot_nn(normed, inward[...]).astype(LOW)
    stores[1].start()
    masks = head_masks()
    for w in range(2):
        rows = slice(144 * w, 144 * w + 144)
        allowed = column_labels[w] == row_labels[w]
        for t in range(4):
            query = projected[rows, 128 * t : 128 * t + 128]
            key = projected[rows, 512 + 128 * t : 640 + 128 * t]
            value_t = projected[rows, 1024 + 128 * t : 1152 + 128 * t].T
            parts = []
            for h in range(4):
                scores = dot_nt(key * masks[h], query) * SCALE
                scores = jnp.where(allowed, scores, -1e30)
                weights = jnp.exp(scores - jnp.max(scores, axis=0, keepdims=True))
                share = weights * (1.0 / jnp.sum(weights, axis=0, keepdims=True))
                share = share.astype(LOW)
                attention[w, 4 * t + h] = share
                parts.append(dot_nn(value_t[32 * h : 32 * h + 32], share))
            attended[rows, 128 * t : 128 * t + 128] = jnp.concatenate(parts, axis=0).T.astype(LOW)
            heads = pl.ds(4 * t, 4)
            store = pltpu.make_async_copy(attention.at[w, heads], far_attention.at[w, heads], shares_out.at[w, t])
            store.start()
            stores.append(store)
    fetches[1].wait()
    result = (values + dot_nn(attended[...], outward[...])).astype(LOW)
    natural = gather(table, FROM_WINDOWS, {0: result})
    block[...] = natural.astype(LOW)
    last_row[...] = jnp.concatenate([natural[120:144], natural[264:]], axis=0).astype(LOW)
    cell_parts = {1: cells[:, :512], 2: cells[:, 512:]} | arrived_parts
    shift_cotangent(core, table, cell_parts, shifted, kept, sent, columns, picked)
    for store in stores:
        store.wait()


def merge_kernel(table, block, prior, upstream, columns, other_columns, normed, bundle, far_back, back_row, back, back_out):
    merged = gather(table, TO_CELLS, {0: block[...], 1: prior[...]})
    pieces = [merged[72 * k : 72 * k + 72] for k in range(4)]
    exact, inverse_std = normalize(jnp.concatenate(pieces, axis=1))
    grads = upstream[...]
    grads = inverse_std * (
        grads
        - jnp.mean(grads, axis=-1, keepdims=True)
        - exact * jnp.mean(grads * exact, axis=-1, keepdims=True)
    )
    stacked = jnp.concatenate([grads[:, 512 * k : 512 * k + 512] for k in range(4)], axis=0)
    stacked = stacked.astype(LOW)
    positions = gather(table, FROM_CELLS, {0: stacked})
    back[...] = positions[:288].astype(LOW)
    store = pltpu.make_async_copy(back, far_back, back_out)
    store.start()
    back_row[...] = positions[288:].astype(LOW)
    normed[...] = exact.astype(LOW)
    for k in range(8):
        bundle[k, 0] = columns[k % 2]
        bundle[k, 1] = other_columns[k % 2]
        for half in range(2):
            at = 512 * (k // 2) + 256 * half
            bundle[k, 2 + half] = exact[:, at : at + 256].astype(LOW)
    store.wait()


def merging_kernel(xh, bundle, other_normed, kept, sent, total):
    for half in range(2):
        terms = 0.0
        for k in range(8):
            terms += dot_tn(bundle[k, 0], bundle[k, 2 + half]) + dot_tn(bundle[k, 1], other_normed[k, half])
        terms = terms.astype(LOW)
        for m in range(16):
            total[32 * m + 16 * half : 32 * m + 16 * half + 16] = terms[16 * m : 16 * m + 16]
    kept[...] = total[pl.ds(pl.multiple_of(256 * xh[0], 256), 256)]
    sent[...] = total[pl.ds(pl.multiple_of(256 - 256 * xh[0], 256), 256)]


def backward_kernel(
    core, table, back, next_row, windows, projected, far_attention, attended, far_inward, outward,
    token_grads, far_kept, far_sent,
    projected_back, inward_t, outward_t, attention, inward, kept, sent, shares_in, weight_in, terms_out,
):
    loads = [pltpu.make_async_copy(far_attention.at[w], attention.at[w], shares_in.at[w]) for w in range(2)]
    loads.append(pltpu.make_async_copy(far_inward, inward, weight_in))
    for load in loads:
        load.start()
    upstream = gather(table, UPSTREAM, {0: back[...], 1: next_row[...]})
    upstream_low = upstream.astype(LOW)
    attended_back = dot_nt(upstream_low, outward[...]).astype(LOW)
    masks = head_masks()
    for w in range(2):
        rows = slice(144 * w, 144 * w + 144)
        loads[w].wait()
        for t in range(4):
            query = projected[rows, 128 * t : 128 * t + 128]
            key_t = projected[rows, 512 + 128 * t : 640 + 128 * t].T
            value = projected[rows, 1024 + 128 * t : 1152 + 128 * t]
            grads = attended_back[rows, 128 * t : 128 * t + 128]
            query_parts, key_back, value_back = [], 0.0, 0.0
            for h in range(4):
                low = attention[w, 4 * t + h]
                share = low.astype(WIDE)
                product = share * dot_nt(value * masks[h], grads)
                total = jnp.sum(product, axis=0, keepdims=True)
                score_back = ((product - share * total) * SCALE).astype(LOW)
                value_back += dot_nn(low, grads * masks[h])
                key_back += dot_nn(score_back, query * masks[h])
                query_parts.append(dot_nn(key_t[32 * h : 32 * h + 32], score_back))
            query_back = jnp.concatenate(query_parts, axis=0).T
            projected_back[rows, 128 * t : 128 * t + 128] = query_back.astype(LOW)
            projected_back[rows, 512 + 128 * t : 640 + 128 * t] = key_back.astype(LOW)
            projected_back[rows, 1024 + 128 * t : 1152 + 128 * t] = value_back.astype(LOW)
    normed, inverse_std = normalize(windows[...].astype(WIDE))
    normed_low = normed.astype(LOW)
    for j in range(4):
        inward_t[384 * j : 384 * j + 384] = dot_tn(projected_back[:, 384 * j : 384 * j + 384], normed_low).astype(LOW)
    outward_t[...] = dot_tn(upstream_low, attended[...]).astype(LOW)
    mine = core[0]
    for place in range(16):
        for terms, parity in ((kept, mine), (sent, 1 - mine)):
            at = 2 * place + parity
            for k in range(4):
                lanes = slice(128 * k, 128 * k + 128)
                head = pl.ds(pl.multiple_of(48 * at, 16), 32)
                tail = pl.ds(pl.multiple_of(48 * at + 32, 16), 16)
                last = pl.ds(pl.multiple_of(16 * at, 16), 16)
                terms[place // 8, k, 0, place % 8] = inward_t[head, lanes]
                terms[place // 8, k, 1, place % 8, 0:16] = inward_t[tail, lanes]
                terms[place // 8, k, 1, place % 8, 16:32] = outward_t[last, lanes]
    stores = [
        pltpu.make_async_copy(sent, far_sent, terms_out.at[0]),
        pltpu.make_async_copy(kept, far_kept, terms_out.at[1]),
    ]
    for store in stores:
        store.start()
    loads[2].wait()
    normed_back = dot_nt(projected_back[...], inward[...])
    branch = inverse_std * (
        normed_back
        - jnp.mean(normed_back, axis=-1, keepdims=True)
        - normed * jnp.mean(normed_back * normed, axis=-1, keepdims=True)
    )
    result = (upstream + branch.astype(LOW).astype(WIDE)).astype(LOW)
    token_grads[...] = gather(table, FROM_WINDOWS, {0: result}).astype(LOW)
    for store in stores:
        store.wait()


def shares_kernel(shares, inward_grads, outward_grads, merging_grads):
    for k in range(4):
        lanes = slice(128 * k, 128 * k + 128)
        inward_grads[0:32, lanes] = shares[2 * k, :, :128].astype(WIDE)
        inward_grads[32:48, lanes] = shares[2 * k + 1, 0:16, :128].astype(WIDE)
        outward_grads[:, lanes] = shares[2 * k + 1, 16:32, :128].astype(WIDE)
        for g in range(2):
            for half in range(2):
                at = 512 * k + 256 * half
                part = shares[2 * k + g, 16 * half : 16 * half + 16, 128:]
                merging_grads[16 * g : 16 * g + 16, at : at + 256] = part.astype(WIDE)


def call(kernel, outs, *operands, scratch=(), scalars=0, room=8, far=(), far_outs=()):
    specs = [pl.BlockSpec()] * len(operands)
    for at in range(scalars):
        specs[at] = pl.BlockSpec(memory_space=pltpu.SMEM)
    for at in far:
        specs[at] = pl.BlockSpec(memory_space=pltpu.HBM)
    out_specs = [pl.BlockSpec(memory_space=pltpu.HBM) if at in far_outs else pl.BlockSpec() for at in range(len(outs))]
    return pl.pallas_call(
        kernel,
        in_specs=specs,
        out_specs=out_specs,
        out_shape=[
            jax.ShapeDtypeStruct(shape[:-1], WIDE) if shape[-1] is WIDE else jax.ShapeDtypeStruct(shape, LOW)
            for shape in outs
        ],
        scratch_shapes=[pltpu.VMEM(shape, LOW) if isinstance(shape, tuple) else shape for shape in scratch],
        compiler_params=pltpu.CompilerParams(vmem_limit_bytes=room * 1024 * 1024),
    )(*operands)


def from_behind(value, axis, steps):
    count = lax.axis_size(axis)
    pairs = [(source, (source + steps) % count) for source in range(count)]
    return lax.ppermute(value, axis, pairs)


def local_windows(layout):
    return layout.reshape(2, 6, 2, 12).transpose(2, 0, 1, 3).reshape(2, 144)


def to_neighbours(parts, steps):
    grp, lat, both = parts
    pairs = [
        (4 * 0 + 2 * row + level, (row + steps) % 4 * 2 + (level + steps) % 2) for row in range(4) for level in range(2)
    ]
    return (
        from_behind(grp, ("grp",), steps),
        from_behind(lat, ("lat",), steps),
        lax.ppermute(both, ("lat", "grp"), pairs),
    )


PLANES = [(120, 512), (96, 512), (96, 512)]


def shift_forward(table, tokens, cells):
    parts = to_neighbours(call(planes_in_kernel, PLANES, tokens, cells), -1)
    (columns,) = call(columns_in_kernel, [(108, 512)], tokens, cells, *parts)
    return (*parts, from_behind(columns, LON, -1))


def wide_sum(parts):
    return jnp.sum(parts.astype(WIDE), axis=0).astype(LOW)


def over_planes(terms):
    terms = terms.reshape((16,) + terms.shape[3:])
    return wide_sum(lax.all_to_all(terms, ("xh", "lat", "grp"), 0, 0))


def tied(*values):
    return lax.optimization_barrier(values)


def body(fine_tokens, region_ids, inward_weight, outward_weight, merging_weight, coarse_cotangent):
    table = jnp.asarray(TABLE)
    core = lax.axis_index("core").reshape(1)
    tokens = fine_tokens.reshape(288, 512)
    cells = coarse_cotangent.reshape(72, 1024)
    parts = shift_forward(table, tokens, cells)
    labels = local_windows(region_ids)
    block, last_row, windows, projected, attention, attended, shifted, columns, sent_columns = call(
        forward_kernel,
        [
            (288, 512), (48, 512), (288, 512), (288, 1536), (2, HEADS, 144, 144), (288, 512),
            (72, 1024), (2, 72, 256), (2, 72, 256),
        ],
        core, table, tokens, cells, *parts, labels.reshape(2, 1, 144), labels.reshape(2, 144, 1), inward_weight, outward_weight,
        scratch=[
            (512, 1536), (512, 512), (2, HEADS, 144, 144), (1024, 72), (256, 72), (288, 512), (288, 1536),
            pltpu.SemaphoreType.DMA((2,)), pltpu.SemaphoreType.DMA((2, 4)), pltpu.SemaphoreType.DMA((2,)),
        ],
        scalars=1, room=54, far=(10, 11), far_outs=(2, 3, 4),
    )
    prior = from_behind(last_row, ("lat",), 1)
    other_columns = from_behind(sent_columns, ("core",), 1)
    merged_upstream = dot_nt(shifted, merging_weight)
    merged_normed, bundle, back, back_row = call(
        merge_kernel,
        [(72, 2048), (8, 4, 72, 256), (288, 512), (48, 512)],
        table, block, prior, merged_upstream, columns, other_columns,
        scratch=[(288, 512), pltpu.SemaphoreType.DMA], far_outs=(2,),
    )
    next_row = from_behind(back_row, ("lat",), -1)
    next_row, bundle = tied(next_row, bundle)
    bundle = lax.all_to_all(bundle, ("lat", "grp"), 0, 0)
    token_grads, kept, sent = call(
        backward_kernel,
        [(288, 512), (2, 4, 2, 8, 32, 128), (2, 4, 2, 8, 32, 128)],
        core, table, back, next_row, windows, projected, attention, attended, inward_weight, outward_weight,
        scratch=[
            (288, 1536), (1536, 512), (512, 512), (2, HEADS, 144, 144), (512, 1536),
            (2, 4, 2, 8, 32, 128), (2, 4, 2, 8, 32, 128),
            pltpu.SemaphoreType.DMA((2,)), pltpu.SemaphoreType.DMA, pltpu.SemaphoreType.DMA((2,)),
        ],
        scalars=1, room=54, far=(6, 8), far_outs=(1, 2),
    )
    merged_normed, token_grads = tied(merged_normed, token_grads)
    coarse_field = dot_nn(merged_normed, merging_weight).astype(LOW)
    packed = call(planes_out_kernel, PLANES, table, token_grads, coarse_field)
    kept, sent, bundle, *packed = tied(kept, sent, bundle, *packed)
    came = from_behind(sent, ("core",), 1)
    block_terms = (kept.astype(WIDE) + came.astype(WIDE)).astype(LOW)
    parts_out = to_neighbours(packed, 1)
    block_terms, *parts_out = tied(block_terms, *parts_out)
    block_planes = over_planes(block_terms)
    other_normed = from_behind(bundle[:, 2:], ("core",), 1)
    merging_kept, merging_sent = call(
        merging_kernel,
        [(256, 256), (256, 256)],
        lax.axis_index("xh").reshape(1), bundle, other_normed,
        scratch=[(512, 256)], scalars=1,
    )
    merging_came = from_behind(merging_sent, ("xh",), 1)
    (lon_out,) = call(columns_out_kernel, [(108, 512)], table, token_grads, coarse_field, *parts_out)
    lon_out = from_behind(lon_out, LON, 1)
    token_grads, coarse_field = call(
        all_out_kernel, [(288, 512), (72, 1024)], table, token_grads, coarse_field, *parts_out, lon_out
    )
    block_planes, merging_came, coarse_field = tied(block_planes, merging_came, coarse_field)
    merging_planes = (merging_kept.astype(WIDE) + merging_came.astype(WIDE)).astype(LOW).reshape(8, 32, 256)
    planes = jnp.concatenate([block_planes, merging_planes], axis=2)
    share = wide_sum(lax.all_to_all(planes, ("z",), 0, 0))
    shares = lax.all_to_all(jnp.broadcast_to(share[None], (8, 32, 384)), ("lat", "grp"), 0, 0)
    grads = call(shares_kernel, [(48, 512, WIDE), (16, 512, WIDE), (32, 2048, WIDE)], shares)
    return (
        coarse_field.reshape(2, 3, 12, 1024),
        token_grads.reshape(2, 6, 24, 512),
        *(share.T for share in grads),
    )


def solution(mesh):
    fine = Mesh(mesh.devices.reshape(4, 2, 8, 2, 2), ("lat", "xh", "z", "core", "grp"))
    return jax.shard_map(
        body,
        mesh=fine,
        in_specs=(
            P("grp", "lat", LON, None),
            P("grp", "lat", LON),
            P(),
            P(),
            P(),
            P("grp", "lat", LON, None),
        ),
        out_specs=(
            P("grp", "lat", LON, None),
            P("grp", "lat", LON, None),
            P(None, LON),
            P(None, LON),
            P(None, LON),
        ),
        check_vma=False,
    )
```

```python
import jax
import jax.numpy as jnp
import numpy as np
from jax import lax
from jax.experimental import pallas as pl
from jax.experimental.pallas import tpu as pltpu
from jax.sharding import Mesh, PartitionSpec as P

HEADS = 16
LON = ("xh", "z", "core")
SCALE = 32 ** (-0.5)
LOW = jnp.bfloat16
WIDE = jnp.float32


def halves(fields):
    return np.concatenate([fields.reshape(-1), (fields + 1000).reshape(-1)])


def join(*parts):
    return np.concatenate([part.reshape(-1) for part in parts])


FINE_AT = np.arange(288).reshape(2, 6, 24)
CELL_AT = 1000 + np.arange(72).reshape(2, 3, 12)


def arrived(source, rows):
    fine = 1000 * source + np.arange(72).reshape(3, 24)
    cells = 1000 * source + 72 + np.arange(12 * rows).reshape(rows, 12)
    return fine, cells, 12 * rows


def shift_in():
    grp, lat, both = arrived(3, 2), arrived(4, 1), arrived(5, 1)
    first = [
        join(FINE_AT[0, 3:], halves(CELL_AT[0, 1:])),
        join(FINE_AT[1, :3], halves(CELL_AT[1, :1])),
        join(FINE_AT[0, :3], halves(CELL_AT[0, :1])),
    ]
    fine = np.stack([np.concatenate([FINE_AT[1, 3:], lat[0]]), np.concatenate([grp[0], both[0]])])
    left = np.stack([np.concatenate([CELL_AT[1, 1:], lat[1]]), np.concatenate([grp[1], both[1]])])
    right = np.stack(
        [np.concatenate([CELL_AT[1, 1:] + 1000, lat[1] + lat[2]]), np.concatenate([grp[1] + grp[2], both[1] + both[2]])]
    )
    second = join(fine[:, :, :6], left[:, :, :3], right[:, :, :3])
    lon_fine = 6000 + np.arange(72).reshape(2, 6, 6)
    lon_cells = 6072 + np.arange(18).reshape(2, 3, 3)
    fine = np.concatenate([fine[:, :, 6:], lon_fine], axis=2)
    left = np.concatenate([left[:, :, 3:], lon_cells], axis=2)
    right = np.concatenate([right[:, :, 3:], lon_cells + 18], axis=2)
    windows = fine.reshape(2, 6, 2, 12).transpose(2, 0, 1, 3)
    return join(*first), second, windows.reshape(-1), join(left, right)


def shift_out():
    first = join(
        FINE_AT[1, :3], halves(CELL_AT[1, :2]), FINE_AT[0, 3:], halves(CELL_AT[0, 2:]), FINE_AT[1, 3:], halves(CELL_AT[1, 2:])
    )
    grp, lat, both = arrived(3, 2), arrived(4, 1), arrived(5, 1)
    fine = np.stack([np.concatenate([both[0], grp[0]]), np.concatenate([lat[0], FINE_AT[0, :3]])])
    left = np.stack([np.concatenate([both[1], grp[1]]), np.concatenate([lat[1], CELL_AT[0, :2]])])
    right = np.stack(
        [
            np.concatenate([both[1] + both[2], grp[1] + grp[2]]),
            np.concatenate([lat[1] + lat[2], CELL_AT[0, :2] + 1000]),
        ]
    )
    second = join(fine[:, :, 18:], left[:, :, 9:], right[:, :, 9:])
    lon_fine = 6000 + np.arange(72).reshape(2, 6, 6)
    lon_cells = 6072 + np.arange(18).reshape(2, 3, 3)
    fine = np.concatenate([lon_fine, fine[:, :, :18]], axis=2)
    left = np.concatenate([lon_cells, left[:, :, :9]], axis=2)
    right = np.concatenate([lon_cells + 18, right[:, :, :9]], axis=2)
    return first, second, join(fine, left, right)


def block_maps():
    natural = np.arange(288).reshape(2, 6, 24)
    windows = natural.reshape(2, 6, 2, 12).transpose(2, 0, 1, 3).reshape(288)
    extended = np.concatenate([1000 + np.arange(48).reshape(2, 1, 24), natural[:, :5]], axis=1)
    to_cells = extended.reshape(2, 3, 2, 12, 2).transpose(4, 2, 0, 1, 3).reshape(288)
    from_cells = np.full(336, -1)
    from_cells[np.where(to_cells < 1000, to_cells, to_cells - 712)] = np.arange(288)
    replaced = natural.copy()
    replaced[:, 5] = 1000 + np.arange(48).reshape(2, 24)
    return np.argsort(windows), to_cells, from_cells, replaced.reshape(288)[windows]


def row_table():
    columns = [*shift_in(), *shift_out(), *block_maps()]
    table = np.full((432, len(columns)), -1, np.int32)
    for at, column in enumerate(columns):
        table[: len(column), at] = column
    return table


TABLE = row_table()
(
    IN_FIRST, IN_SECOND, IN_WINDOWS, IN_CELLS, OUT_FIRST, OUT_SECOND, OUT_ALL,
    FROM_WINDOWS, TO_CELLS, FROM_CELLS, UPSTREAM,
) = range(11)
ROWS = [int((TABLE[:, at] >= 0).sum()) for at in range(11)]
ROWS[FROM_CELLS] = 336


def gather(table, column, sources):
    return gather_named(table[: ROWS[column], column : column + 1], sources)


def gather_named(names, sources):
    total = 0.0
    for source, value in sources.items():
        place = lax.broadcasted_iota(jnp.int32, (names.shape[0], value.shape[0]), 1) + 1000 * source
        total += dot_nn((names == place).astype(WIDE).astype(LOW), value)
    return total


def dot_nn(a, b):
    return lax.dot_general(a, b, (((1,), (0,)), ((), ())), preferred_element_type=WIDE)


def dot_nt(a, b):
    return lax.dot_general(a, b, (((1,), (1,)), ((), ())), preferred_element_type=WIDE)


def dot_tn(a, b):
    return lax.dot_general(a, b, (((0,), (0,)), ((), ())), preferred_element_type=WIDE)


def head_masks():
    head = lax.broadcasted_iota(jnp.int32, (144, 128), 1) >> 5
    return [(head == h).astype(WIDE).astype(LOW) for h in range(4)]


def normalize(values):
    centred = values - jnp.mean(values, axis=-1, keepdims=True)
    inverse_std = lax.rsqrt(jnp.mean(centred * centred, axis=-1, keepdims=True) + 1e-05)
    return (centred * inverse_std, inverse_std)


def own(tokens, cells):
    return {0: tokens[...], 1: cells[:, :512], 2: cells[:, 512:]}


def arrivals(grp, lat, both):
    return {3: grp[...], 4: lat[...], 5: both[...]}


def store_planes(packed, grp, lat, both):
    grp[...] = packed[:120].astype(LOW)
    lat[...] = packed[120:216].astype(LOW)
    both[...] = packed[216:].astype(LOW)


def runs(target):
    target = np.asarray(target)
    begins = [0] + [at for at in range(1, len(target)) if target[at] != target[at - 1] + 1]
    return [(at, int(target[at]) - at) for at in begins]


def column_names(column):
    row = lax.broadcasted_iota(jnp.int32, (ROWS[column], 1), 0)
    ahead = jnp.zeros_like(row)
    for begin, difference in runs(TABLE[: ROWS[column], column]):
        ahead = jnp.where(row >= begin, difference, ahead)
    return row + ahead


def planes_in_kernel(tokens, cells, *outs):
    store_planes(gather_named(column_names(IN_FIRST), own(tokens, cells)), *outs)


def columns_in_kernel(tokens, cells, grp, lat, both, out):
    sources = own(tokens, cells) | arrivals(grp, lat, both)
    out[...] = gather_named(column_names(IN_SECOND), sources).astype(LOW)


def planes_out_kernel(table, tokens, cells, *outs):
    store_planes(gather(table, OUT_FIRST, own(tokens, cells)), *outs)


def columns_out_kernel(table, tokens, cells, grp, lat, both, out):
    out[...] = gather(table, OUT_SECOND, own(tokens, cells) | arrivals(grp, lat, both)).astype(LOW)


def all_out_kernel(table, tokens, cells, grp, lat, both, lon, fine, coarse):
    packed = gather(table, OUT_ALL, own(tokens, cells) | arrivals(grp, lat, both) | {6: lon[...]})
    fine[...] = packed[:288].astype(LOW)
    coarse[:, :512] = packed[288:360].astype(LOW)
    coarse[:, 512:] = packed[360:].astype(LOW)


def shift_cotangent(core, table, sources, shifted, kept, sent, columns, picked):
    packed = gather(table, IN_CELLS, sources)
    cotangent = jnp.concatenate([packed[:72], packed[72:]], axis=1)
    shifted[...] = cotangent.astype(LOW)
    columns[...] = cotangent.T.astype(LOW)
    for out, parity in ((kept, core[0]), (sent, 1 - core[0])):
        for g in range(2):
            for m in range(16):
                at = pl.multiple_of(64 * m + 32 * parity + 16 * g, 16)
                picked[16 * m : 16 * m + 16] = columns[pl.ds(at, 16)]
            out[g] = picked[...].astype(WIDE).T.astype(LOW)


def forward_kernel(
    core, table, tokens, cells, grp, lat, both, lon, row_labels, column_labels, far_inward, far_outward,
    block, last_row, far_windows, far_projected, far_attention, attended, shifted, kept, sent,
    inward, outward, attention, columns, picked, windows, projected, weights_in, shares_out, early_out,
):
    fetches = [
        pltpu.make_async_copy(far_inward, inward, weights_in.at[0]),
        pltpu.make_async_copy(far_outward, outward, weights_in.at[1]),
    ]
    for copy in fetches:
        copy.start()
    stores = [
        pltpu.make_async_copy(windows, far_windows, early_out.at[0]),
        pltpu.make_async_copy(projected, far_projected, early_out.at[1]),
    ]
    arrived_parts = arrivals(grp, lat, both) | {6: lon[...]}
    values = gather(table, IN_WINDOWS, {0: tokens[...]} | arrived_parts)
    windows[...] = values.astype(LOW)
    stores[0].start()
    normed = normalize(values)[0].astype(LOW)
    fetches[0].wait()
    projected[...] = dot_nn(normed, inward[...]).astype(LOW)
    stores[1].start()
    masks = head_masks()
    for w in range(2):
        rows = slice(144 * w, 144 * w + 144)
        allowed = column_labels[w] == row_labels[w]
        for t in range(4):
            query = projected[rows, 128 * t : 128 * t + 128]
            key = projected[rows, 512 + 128 * t : 640 + 128 * t]
            value_t = projected[rows, 1024 + 128 * t : 1152 + 128 * t].T
            parts = []
            for h in range(4):
                scores = dot_nt(key * masks[h], query) * SCALE
                scores = jnp.where(allowed, scores, -1e30)
                weights = jnp.exp(scores - jnp.max(scores, axis=0, keepdims=True))
                share = weights * (1.0 / jnp.sum(weights, axis=0, keepdims=True))
                share = share.astype(LOW)
                attention[w, 4 * t + h] = share
                parts.append(dot_nn(value_t[32 * h : 32 * h + 32], share))
            attended[rows, 128 * t : 128 * t + 128] = jnp.concatenate(parts, axis=0).T.astype(LOW)
            heads = pl.ds(4 * t, 4)
            store = pltpu.make_async_copy(attention.at[w, heads], far_attention.at[w, heads], shares_out.at[w, t])
            store.start()
            stores.append(store)
    fetches[1].wait()
    result = (values + dot_nn(attended[...], outward[...])).astype(LOW)
    natural = gather(table, FROM_WINDOWS, {0: result})
    block[...] = natural.astype(LOW)
    last_row[...] = jnp.concatenate([natural[120:144], natural[264:]], axis=0).astype(LOW)
    cell_parts = {1: cells[:, :512], 2: cells[:, 512:]} | arrived_parts
    shift_cotangent(core, table, cell_parts, shifted, kept, sent, columns, picked)
    for store in stores:
        store.wait()


def merge_kernel(table, block, prior, upstream, columns, other_columns, normed, bundle, far_back, back_row, back, back_out):
    merged = gather(table, TO_CELLS, {0: block[...], 1: prior[...]})
    pieces = [merged[72 * k : 72 * k + 72] for k in range(4)]
    exact, inverse_std = normalize(jnp.concatenate(pieces, axis=1))
    grads = upstream[...]
    grads = inverse_std * (
        grads
        - jnp.mean(grads, axis=-1, keepdims=True)
        - exact * jnp.mean(grads * exact, axis=-1, keepdims=True)
    )
    stacked = jnp.concatenate([grads[:, 512 * k : 512 * k + 512] for k in range(4)], axis=0)
    stacked = stacked.astype(LOW)
    positions = gather(table, FROM_CELLS, {0: stacked})
    back[...] = positions[:288].astype(LOW)
    store = pltpu.make_async_copy(back, far_back, back_out)
    store.start()
    back_row[...] = positions[288:].astype(LOW)
    normed[...] = exact.astype(LOW)
    for k in range(8):
        bundle[k, 0] = columns[k % 2]
        bundle[k, 1] = other_columns[k % 2]
        for half in range(2):
            at = 512 * (k // 2) + 256 * half
            bundle[k, 2 + half] = exact[:, at : at + 256].astype(LOW)
    store.wait()


def merging_kernel(xh, bundle, other_normed, kept, sent, total):
    for half in range(2):
        terms = 0.0
        for k in range(8):
            terms += dot_tn(bundle[k, 0], bundle[k, 2 + half]) + dot_tn(bundle[k, 1], other_normed[k, half])
        terms = terms.astype(LOW)
        for m in range(16):
            total[32 * m + 16 * half : 32 * m + 16 * half + 16] = terms[16 * m : 16 * m + 16]
    kept[...] = total[pl.ds(pl.multiple_of(256 * xh[0], 256), 256)]
    sent[...] = total[pl.ds(pl.multiple_of(256 - 256 * xh[0], 256), 256)]


def backward_kernel(
    core, table, back, next_row, windows, projected, far_attention, attended, far_inward, outward,
    token_grads, far_kept, far_sent,
    projected_back, inward_t, outward_t, attention, inward, kept, sent, shares_in, weight_in, terms_out,
):
    loads = [pltpu.make_async_copy(far_attention.at[w], attention.at[w], shares_in.at[w]) for w in range(2)]
    loads.append(pltpu.make_async_copy(far_inward, inward, weight_in))
    for load in loads:
        load.start()
    upstream = gather(table, UPSTREAM, {0: back[...], 1: next_row[...]})
    upstream_low = upstream.astype(LOW)
    attended_back = dot_nt(upstream_low, outward[...]).astype(LOW)
    masks = head_masks()
    for w in range(2):
        rows = slice(144 * w, 144 * w + 144)
        loads[w].wait()
        for t in range(4):
            query = projected[rows, 128 * t : 128 * t + 128]
            key_t = projected[rows, 512 + 128 * t : 640 + 128 * t].T
            value = projected[rows, 1024 + 128 * t : 1152 + 128 * t]
            grads = attended_back[rows, 128 * t : 128 * t + 128]
            query_parts, key_back, value_back = [], 0.0, 0.0
            for h in range(4):
                low = attention[w, 4 * t + h]
                share = low.astype(WIDE)
                product = share * dot_nt(value * masks[h], grads)
                total = jnp.sum(product, axis=0, keepdims=True)
                score_back = ((product - share * total) * SCALE).astype(LOW)
                value_back += dot_nn(low, grads * masks[h])
                key_back += dot_nn(score_back, query * masks[h])
                query_parts.append(dot_nn(key_t[32 * h : 32 * h + 32], score_back))
            query_back = jnp.concatenate(query_parts, axis=0).T
            projected_back[rows, 128 * t : 128 * t + 128] = query_back.astype(LOW)
            projected_back[rows, 512 + 128 * t : 640 + 128 * t] = key_back.astype(LOW)
            projected_back[rows, 1024 + 128 * t : 1152 + 128 * t] = value_back.astype(LOW)
    normed, inverse_std = normalize(windows[...].astype(WIDE))
    normed_low = normed.astype(LOW)
    for j in range(4):
        inward_t[384 * j : 384 * j + 384] = dot_tn(projected_back[:, 384 * j : 384 * j + 384], normed_low).astype(LOW)
    outward_t[...] = dot_tn(upstream_low, attended[...]).astype(LOW)
    mine = core[0]
    for place in range(16):
        for terms, parity in ((kept, mine), (sent, 1 - mine)):
            at = 2 * place + parity
            for k in range(4):
                lanes = slice(128 * k, 128 * k + 128)
                head = pl.ds(pl.multiple_of(48 * at, 16), 32)
                tail = pl.ds(pl.multiple_of(48 * at + 32, 16), 16)
                last = pl.ds(pl.multiple_of(16 * at, 16), 16)
                terms[place // 8, k, 0, place % 8] = inward_t[head, lanes]
                terms[place // 8, k, 1, place % 8, 0:16] = inward_t[tail, lanes]
                terms[place // 8, k, 1, place % 8, 16:32] = outward_t[last, lanes]
    stores = [
        pltpu.make_async_copy(sent, far_sent, terms_out.at[0]),
        pltpu.make_async_copy(kept, far_kept, terms_out.at[1]),
    ]
    for store in stores:
        store.start()
    loads[2].wait()
    normed_back = dot_nt(projected_back[...], inward[...])
    branch = inverse_std * (
        normed_back
        - jnp.mean(normed_back, axis=-1, keepdims=True)
        - normed * jnp.mean(normed_back * normed, axis=-1, keepdims=True)
    )
    result = (upstream + branch.astype(LOW).astype(WIDE)).astype(LOW)
    token_grads[...] = gather(table, FROM_WINDOWS, {0: result}).astype(LOW)
    for store in stores:
        store.wait()


def shares_kernel(shares, inward_grads, outward_grads, merging_grads):
    for k in range(4):
        lanes = slice(128 * k, 128 * k + 128)
        inward_grads[0:32, lanes] = shares[2 * k, :, :128].astype(WIDE)
        inward_grads[32:48, lanes] = shares[2 * k + 1, 0:16, :128].astype(WIDE)
        outward_grads[:, lanes] = shares[2 * k + 1, 16:32, :128].astype(WIDE)
        for g in range(2):
            for half in range(2):
                at = 512 * k + 256 * half
                part = shares[2 * k + g, 16 * half : 16 * half + 16, 128:]
                merging_grads[16 * g : 16 * g + 16, at : at + 256] = part.astype(WIDE)


def call(kernel, outs, *operands, scratch=(), scalars=0, room=8, far=(), far_outs=()):
    specs = [pl.BlockSpec()] * len(operands)
    for at in range(scalars):
        specs[at] = pl.BlockSpec(memory_space=pltpu.SMEM)
    for at in far:
        specs[at] = pl.BlockSpec(memory_space=pltpu.HBM)
    out_specs = [pl.BlockSpec(memory_space=pltpu.HBM) if at in far_outs else pl.BlockSpec() for at in range(len(outs))]
    return pl.pallas_call(
        kernel,
        in_specs=specs,
        out_specs=out_specs,
        out_shape=[
            jax.ShapeDtypeStruct(shape[:-1], WIDE) if shape[-1] is WIDE else jax.ShapeDtypeStruct(shape, LOW)
            for shape in outs
        ],
        scratch_shapes=[pltpu.VMEM(shape, LOW) if isinstance(shape, tuple) else shape for shape in scratch],
        compiler_params=pltpu.CompilerParams(vmem_limit_bytes=room * 1024 * 1024),
    )(*operands)


def from_behind(value, axis, steps):
    count = lax.axis_size(axis)
    pairs = [(source, (source + steps) % count) for source in range(count)]
    return lax.ppermute(value, axis, pairs)


def local_windows(layout):
    return layout.reshape(2, 6, 2, 12).transpose(2, 0, 1, 3).reshape(2, 144)


def to_neighbours(parts, steps):
    grp, lat, both = parts
    pairs = [
        (4 * 0 + 2 * row + level, (row + steps) % 4 * 2 + (level + steps) % 2) for row in range(4) for level in range(2)
    ]
    return (
        from_behind(grp, ("grp",), steps),
        from_behind(lat, ("lat",), steps),
        lax.ppermute(both, ("lat", "grp"), pairs),
    )


PLANES = [(120, 512), (96, 512), (96, 512)]


def shift_forward(table, tokens, cells):
    parts = to_neighbours(call(planes_in_kernel, PLANES, tokens, cells), -1)
    (columns,) = call(columns_in_kernel, [(108, 512)], tokens, cells, *parts)
    return (*parts, from_behind(columns, LON, -1))


def wide_sum(parts):
    return jnp.sum(parts.astype(WIDE), axis=0).astype(LOW)


def over_planes(terms):
    terms = terms.reshape((16,) + terms.shape[3:])
    return wide_sum(lax.all_to_all(terms, ("xh", "lat", "grp"), 0, 0))


def tied(*values):
    return lax.optimization_barrier(values)


def body(fine_tokens, region_ids, inward_weight, outward_weight, merging_weight, coarse_cotangent):
    table = jnp.asarray(TABLE)
    core = lax.axis_index("core").reshape(1)
    tokens = fine_tokens.reshape(288, 512)
    cells = coarse_cotangent.reshape(72, 1024)
    parts = shift_forward(table, tokens, cells)
    labels = local_windows(region_ids)
    block, last_row, windows, projected, attention, attended, shifted, columns, sent_columns = call(
        forward_kernel,
        [
            (288, 512), (48, 512), (288, 512), (288, 1536), (2, HEADS, 144, 144), (288, 512),
            (72, 1024), (2, 72, 256), (2, 72, 256),
        ],
        core, table, tokens, cells, *parts, labels.reshape(2, 1, 144), labels.reshape(2, 144, 1), inward_weight, outward_weight,
        scratch=[
            (512, 1536), (512, 512), (2, HEADS, 144, 144), (1024, 72), (256, 72), (288, 512), (288, 1536),
            pltpu.SemaphoreType.DMA((2,)), pltpu.SemaphoreType.DMA((2, 4)), pltpu.SemaphoreType.DMA((2,)),
        ],
        scalars=1, room=54, far=(10, 11), far_outs=(2, 3, 4),
    )
    prior = from_behind(last_row, ("lat",), 1)
    other_columns = from_behind(sent_columns, ("core",), 1)
    merged_upstream = dot_nt(shifted, merging_weight)
    merged_normed, bundle, back, back_row = call(
        merge_kernel,
        [(72, 2048), (8, 4, 72, 256), (288, 512), (48, 512)],
        table, block, prior, merged_upstream, columns, other_columns,
        scratch=[(288, 512), pltpu.SemaphoreType.DMA], far_outs=(2,),
    )
    next_row = from_behind(back_row, ("lat",), -1)
    next_row, bundle = tied(next_row, bundle)
    bundle = lax.all_to_all(bundle, ("lat", "grp"), 0, 0)
    token_grads, kept, sent = call(
        backward_kernel,
        [(288, 512), (2, 4, 2, 8, 32, 128), (2, 4, 2, 8, 32, 128)],
        core, table, back, next_row, windows, projected, attention, attended, inward_weight, outward_weight,
        scratch=[
            (288, 1536), (1536, 512), (512, 512), (2, HEADS, 144, 144), (512, 1536),
            (2, 4, 2, 8, 32, 128), (2, 4, 2, 8, 32, 128),
            pltpu.SemaphoreType.DMA((2,)), pltpu.SemaphoreType.DMA, pltpu.SemaphoreType.DMA((2,)),
        ],
        scalars=1, room=54, far=(6, 8), far_outs=(1, 2),
    )
    merged_normed, token_grads = tied(merged_normed, token_grads)
    coarse_field = dot_nn(merged_normed, merging_weight).astype(LOW)
    packed = call(planes_out_kernel, PLANES, table, token_grads, coarse_field)
    kept, sent, bundle, *packed = tied(kept, sent, bundle, *packed)
    came = from_behind(sent, ("core",), 1)
    block_terms = (kept.astype(WIDE) + came.astype(WIDE)).astype(LOW)
    parts_out = to_neighbours(packed, 1)
    block_planes = over_planes(block_terms)
    other_normed = from_behind(bundle[:, 2:], ("core",), 1)
    merging_kept, merging_sent = call(
        merging_kernel,
        [(256, 256), (256, 256)],
        lax.axis_index("xh").reshape(1), bundle, other_normed,
        scratch=[(512, 256)], scalars=1,
    )
    merging_came = from_behind(merging_sent, ("xh",), 1)
    block_planes, merging_came, grp_out, lat_out = tied(block_planes, merging_came, *parts_out[:2])
    parts_out = (grp_out, lat_out, parts_out[2])
    (lon_out,) = call(columns_out_kernel, [(108, 512)], table, token_grads, coarse_field, *parts_out)
    merging_planes = (merging_kept.astype(WIDE) + merging_came.astype(WIDE)).astype(LOW).reshape(8, 32, 256)
    planes = jnp.concatenate([block_planes, merging_planes], axis=2)
    share = wide_sum(lax.all_to_all(planes, ("z",), 0, 0))
    lon_out = from_behind(lon_out, LON, 1)
    share, lon_out = tied(share, lon_out)
    token_grads, coarse_field = call(
        all_out_kernel, [(288, 512), (72, 1024)], table, token_grads, coarse_field, *parts_out, lon_out
    )
    shares = lax.all_to_all(jnp.broadcast_to(share[None], (8, 32, 384)), ("lat", "grp"), 0, 0)
    grads = call(shares_kernel, [(48, 512, WIDE), (16, 512, WIDE), (32, 2048, WIDE)], shares)
    return (
        coarse_field.reshape(2, 3, 12, 1024),
        token_grads.reshape(2, 6, 24, 512),
        *(share.T for share in grads),
    )


def solution(mesh):
    fine = Mesh(mesh.devices.reshape(4, 2, 8, 2, 2), ("lat", "xh", "z", "core", "grp"))
    return jax.shard_map(
        body,
        mesh=fine,
        in_specs=(
            P("grp", "lat", LON, None),
            P("grp", "lat", LON),
            P(),
            P(),
            P(),
            P("grp", "lat", LON, None),
        ),
        out_specs=(
            P("grp", "lat", LON, None),
            P("grp", "lat", LON, None),
            P(None, LON),
            P(None, LON),
            P(None, LON),
        ),
        check_vma=False,
    )
```

```python
import jax
import jax.numpy as jnp
import numpy as np
from jax import lax
from jax.experimental import pallas as pl
from jax.experimental.pallas import tpu as pltpu
from jax.sharding import Mesh, PartitionSpec as P

HEADS = 16
LON = ("xh", "z", "core")
SCALE = 32 ** (-0.5)
LOW = jnp.bfloat16
WIDE = jnp.float32


def halves(fields):
    return np.concatenate([fields.reshape(-1), (fields + 1000).reshape(-1)])


def join(*parts):
    return np.concatenate([part.reshape(-1) for part in parts])


FINE_AT = np.arange(288).reshape(2, 6, 24)
CELL_AT = 1000 + np.arange(72).reshape(2, 3, 12)


def arrived(source, rows):
    fine = 1000 * source + np.arange(72).reshape(3, 24)
    cells = 1000 * source + 72 + np.arange(12 * rows).reshape(rows, 12)
    return fine, cells, 12 * rows


def shift_in():
    grp, lat, both = arrived(3, 2), arrived(4, 1), arrived(5, 1)
    first = [
        join(FINE_AT[0, 3:], halves(CELL_AT[0, 1:])),
        join(FINE_AT[1, :3], halves(CELL_AT[1, :1])),
        join(FINE_AT[0, :3], halves(CELL_AT[0, :1])),
    ]
    fine = np.stack([np.concatenate([FINE_AT[1, 3:], lat[0]]), np.concatenate([grp[0], both[0]])])
    left = np.stack([np.concatenate([CELL_AT[1, 1:], lat[1]]), np.concatenate([grp[1], both[1]])])
    right = np.stack(
        [np.concatenate([CELL_AT[1, 1:] + 1000, lat[1] + lat[2]]), np.concatenate([grp[1] + grp[2], both[1] + both[2]])]
    )
    second = join(fine[:, :, :6], left[:, :, :3], right[:, :, :3])
    lon_fine = 6000 + np.arange(72).reshape(2, 6, 6)
    lon_cells = 6072 + np.arange(18).reshape(2, 3, 3)
    fine = np.concatenate([fine[:, :, 6:], lon_fine], axis=2)
    left = np.concatenate([left[:, :, 3:], lon_cells], axis=2)
    right = np.concatenate([right[:, :, 3:], lon_cells + 18], axis=2)
    windows = fine.reshape(2, 6, 2, 12).transpose(2, 0, 1, 3)
    return join(*first), second, windows.reshape(-1), join(left, right)


def shift_out():
    first = join(FINE_AT[:, :, 18:], CELL_AT[:, :, 9:], CELL_AT[:, :, 9:] + 1000)
    lon_fine = 6000 + np.arange(72).reshape(2, 6, 6)
    lon_cells = 6072 + np.arange(18).reshape(2, 3, 3)
    fine = np.concatenate([lon_fine, FINE_AT[:, :, :18]], axis=2)
    left = np.concatenate([lon_cells, CELL_AT[:, :, :9]], axis=2)
    right = np.concatenate([lon_cells + 18, CELL_AT[:, :, :9] + 1000], axis=2)
    second = join(
        fine[1, :3], left[1, :2], right[1, :2], fine[0, 3:], left[0, 2], right[0, 2], fine[1, 3:], left[1, 2], right[1, 2]
    )
    grp, lat, both = arrived(3, 2), arrived(4, 1), arrived(5, 1)
    fine = np.stack([np.concatenate([both[0], grp[0]]), np.concatenate([lat[0], fine[0, :3]])])
    left = np.stack([np.concatenate([both[1], grp[1]]), np.concatenate([lat[1], left[0, :2]])])
    right = np.stack(
        [np.concatenate([both[1] + both[2], grp[1] + grp[2]]), np.concatenate([lat[1] + lat[2], right[0, :2]])]
    )
    return first, second, join(fine, left, right)


def block_maps():
    natural = np.arange(288).reshape(2, 6, 24)
    windows = natural.reshape(2, 6, 2, 12).transpose(2, 0, 1, 3).reshape(288)
    extended = np.concatenate([1000 + np.arange(48).reshape(2, 1, 24), natural[:, :5]], axis=1)
    to_cells = extended.reshape(2, 3, 2, 12, 2).transpose(4, 2, 0, 1, 3).reshape(288)
    from_cells = np.full(336, -1)
    from_cells[np.where(to_cells < 1000, to_cells, to_cells - 712)] = np.arange(288)
    replaced = natural.copy()
    replaced[:, 5] = 1000 + np.arange(48).reshape(2, 24)
    return np.argsort(windows), to_cells, from_cells, replaced.reshape(288)[windows]


def row_table():
    columns = [*shift_in(), *shift_out(), *block_maps()]
    table = np.full((432, len(columns)), -1, np.int32)
    for at, column in enumerate(columns):
        table[: len(column), at] = column
    return table


TABLE = row_table()
(
    IN_FIRST, IN_SECOND, IN_WINDOWS, IN_CELLS, OUT_FIRST, OUT_SECOND, OUT_ALL,
    FROM_WINDOWS, TO_CELLS, FROM_CELLS, UPSTREAM,
) = range(11)
ROWS = [int((TABLE[:, at] >= 0).sum()) for at in range(11)]
ROWS[FROM_CELLS] = 336


def gather(table, column, sources):
    return gather_named(table[: ROWS[column], column : column + 1], sources)


def gather_named(names, sources):
    total = 0.0
    for source, value in sources.items():
        place = lax.broadcasted_iota(jnp.int32, (names.shape[0], value.shape[0]), 1) + 1000 * source
        total += dot_nn((names == place).astype(WIDE).astype(LOW), value)
    return total


def dot_nn(a, b):
    return lax.dot_general(a, b, (((1,), (0,)), ((), ())), preferred_element_type=WIDE)


def dot_nt(a, b):
    return lax.dot_general(a, b, (((1,), (1,)), ((), ())), preferred_element_type=WIDE)


def dot_tn(a, b):
    return lax.dot_general(a, b, (((0,), (0,)), ((), ())), preferred_element_type=WIDE)


def head_masks():
    head = lax.broadcasted_iota(jnp.int32, (144, 128), 1) >> 5
    return [(head == h).astype(WIDE).astype(LOW) for h in range(4)]


def normalize(values):
    centred = values - jnp.mean(values, axis=-1, keepdims=True)
    inverse_std = lax.rsqrt(jnp.mean(centred * centred, axis=-1, keepdims=True) + 1e-05)
    return (centred * inverse_std, inverse_std)


def own(tokens, cells):
    return {0: tokens[...], 1: cells[:, :512], 2: cells[:, 512:]}


def arrivals(grp, lat, both):
    return {3: grp[...], 4: lat[...], 5: both[...]}


def store_planes(packed, grp, lat, both):
    grp[...] = packed[:120].astype(LOW)
    lat[...] = packed[120:216].astype(LOW)
    both[...] = packed[216:].astype(LOW)


def runs(target):
    target = np.asarray(target)
    begins = [0] + [at for at in range(1, len(target)) if target[at] != target[at - 1] + 1]
    return [(at, int(target[at]) - at) for at in begins]


def column_names(column):
    row = lax.broadcasted_iota(jnp.int32, (ROWS[column], 1), 0)
    ahead = jnp.zeros_like(row)
    for begin, difference in runs(TABLE[: ROWS[column], column]):
        ahead = jnp.where(row >= begin, difference, ahead)
    return row + ahead


def planes_in_kernel(tokens, cells, *outs):
    store_planes(gather_named(column_names(IN_FIRST), own(tokens, cells)), *outs)


def columns_in_kernel(tokens, cells, grp, lat, both, out):
    sources = own(tokens, cells) | arrivals(grp, lat, both)
    out[...] = gather_named(column_names(IN_SECOND), sources).astype(LOW)


def columns_out_kernel(table, tokens, cells, out):
    out[...] = gather(table, OUT_FIRST, own(tokens, cells)).astype(LOW)


def planes_out_kernel(table, tokens, cells, lon, *outs):
    store_planes(gather(table, OUT_SECOND, own(tokens, cells) | {6: lon[...]}), *outs)


def all_out_kernel(table, tokens, cells, grp, lat, both, lon, fine, coarse):
    packed = gather(table, OUT_ALL, own(tokens, cells) | arrivals(grp, lat, both) | {6: lon[...]})
    fine[...] = packed[:288].astype(LOW)
    coarse[:, :512] = packed[288:360].astype(LOW)
    coarse[:, 512:] = packed[360:].astype(LOW)


def shift_cotangent(core, table, sources, shifted, kept, sent, columns, picked):
    packed = gather(table, IN_CELLS, sources)
    cotangent = jnp.concatenate([packed[:72], packed[72:]], axis=1)
    shifted[...] = cotangent.astype(LOW)
    columns[...] = cotangent.T.astype(LOW)
    for out, parity in ((kept, core[0]), (sent, 1 - core[0])):
        for g in range(2):
            for m in range(16):
                at = pl.multiple_of(64 * m + 32 * parity + 16 * g, 16)
                picked[16 * m : 16 * m + 16] = columns[pl.ds(at, 16)]
            out[g] = picked[...].astype(WIDE).T.astype(LOW)


def forward_kernel(
    core, table, tokens, cells, grp, lat, both, lon, row_labels, column_labels, far_inward, far_outward,
    block, last_row, windows, projected, far_attention, attended, shifted, kept, sent,
    inward, outward, attention, columns, picked, weights_in, shares_out,
):
    fetches = [
        pltpu.make_async_copy(far_inward, inward, weights_in.at[0]),
        pltpu.make_async_copy(far_outward, outward, weights_in.at[1]),
    ]
    for copy in fetches:
        copy.start()
    stores = []
    arrived_parts = arrivals(grp, lat, both) | {6: lon[...]}
    values = gather(table, IN_WINDOWS, {0: tokens[...]} | arrived_parts)
    windows[...] = values.astype(LOW)
    normed = normalize(values)[0].astype(LOW)
    fetches[0].wait()
    projected[...] = dot_nn(normed, inward[...]).astype(LOW)
    masks = head_masks()
    for w in range(2):
        rows = slice(144 * w, 144 * w + 144)
        allowed = column_labels[w] == row_labels[w]
        for t in range(4):
            query = projected[rows, 128 * t : 128 * t + 128]
            key = projected[rows, 512 + 128 * t : 640 + 128 * t]
            value_t = projected[rows, 1024 + 128 * t : 1152 + 128 * t].T
            parts = []
            for h in range(4):
                scores = dot_nt(key * masks[h], query) * SCALE
                scores = jnp.where(allowed, scores, -1e30)
                weights = jnp.exp(scores - jnp.max(scores, axis=0, keepdims=True))
                share = weights * (1.0 / jnp.sum(weights, axis=0, keepdims=True))
                share = share.astype(LOW)
                attention[w, 4 * t + h] = share
                parts.append(dot_nn(value_t[32 * h : 32 * h + 32], share))
            attended[rows, 128 * t : 128 * t + 128] = jnp.concatenate(parts, axis=0).T.astype(LOW)
            heads = pl.ds(4 * t, 4)
            store = pltpu.make_async_copy(attention.at[w, heads], far_attention.at[w, heads], shares_out.at[w, t])
            store.start()
            stores.append(store)
    fetches[1].wait()
    result = (values + dot_nn(attended[...], outward[...])).astype(LOW)
    natural = gather(table, FROM_WINDOWS, {0: result})
    block[...] = natural.astype(LOW)
    last_row[...] = jnp.concatenate([natural[120:144], natural[264:]], axis=0).astype(LOW)
    cell_parts = {1: cells[:, :512], 2: cells[:, 512:]} | arrived_parts
    shift_cotangent(core, table, cell_parts, shifted, kept, sent, columns, picked)
    for store in stores:
        store.wait()


def merge_kernel(table, block, prior, upstream, columns, other_columns, normed, bundle, back, back_row):
    merged = gather(table, TO_CELLS, {0: block[...], 1: prior[...]})
    pieces = [merged[72 * k : 72 * k + 72] for k in range(4)]
    exact, inverse_std = normalize(jnp.concatenate(pieces, axis=1))
    normed[...] = exact.astype(LOW)
    for k in range(8):
        bundle[k, 0] = columns[k % 2]
        bundle[k, 1] = other_columns[k % 2]
        for half in range(2):
            at = 512 * (k // 2) + 256 * half
            bundle[k, 2 + half] = exact[:, at : at + 256].astype(LOW)
    grads = upstream[...]
    grads = inverse_std * (
        grads
        - jnp.mean(grads, axis=-1, keepdims=True)
        - exact * jnp.mean(grads * exact, axis=-1, keepdims=True)
    )
    stacked = jnp.concatenate([grads[:, 512 * k : 512 * k + 512] for k in range(4)], axis=0)
    stacked = stacked.astype(LOW)
    positions = gather(table, FROM_CELLS, {0: stacked})
    back[...] = positions[:288].astype(LOW)
    back_row[...] = positions[288:].astype(LOW)


def merging_kernel(xh, bundle, other_normed, kept, sent, total):
    for half in range(2):
        terms = 0.0
        for k in range(8):
            terms += dot_tn(bundle[k, 0], bundle[k, 2 + half]) + dot_tn(bundle[k, 1], other_normed[k, half])
        terms = terms.astype(LOW)
        for m in range(16):
            total[32 * m + 16 * half : 32 * m + 16 * half + 16] = terms[16 * m : 16 * m + 16]
    kept[...] = total[pl.ds(pl.multiple_of(256 * xh[0], 256), 256)]
    sent[...] = total[pl.ds(pl.multiple_of(256 - 256 * xh[0], 256), 256)]


def backward_kernel(
    core, table, back, next_row, windows, projected, far_attention, attended, far_inward, outward,
    token_grads, kept, sent, projected_back, inward_t, outward_t, attention, inward, shares_in, weight_in,
):
    loads = [pltpu.make_async_copy(far_attention.at[w], attention.at[w], shares_in.at[w]) for w in range(2)]
    loads.append(pltpu.make_async_copy(far_inward, inward, weight_in))
    for load in loads:
        load.start()
    upstream = gather(table, UPSTREAM, {0: back[...], 1: next_row[...]})
    upstream_low = upstream.astype(LOW)
    attended_back = dot_nt(upstream_low, outward[...]).astype(LOW)
    masks = head_masks()
    for w in range(2):
        rows = slice(144 * w, 144 * w + 144)
        loads[w].wait()
        for t in range(4):
            query = projected[rows, 128 * t : 128 * t + 128]
            key_t = projected[rows, 512 + 128 * t : 640 + 128 * t].T
            value = projected[rows, 1024 + 128 * t : 1152 + 128 * t]
            grads = attended_back[rows, 128 * t : 128 * t + 128]
            query_parts, key_back, value_back = [], 0.0, 0.0
            for h in range(4):
                low = attention[w, 4 * t + h]
                share = low.astype(WIDE)
                product = share * dot_nt(value * masks[h], grads)
                total = jnp.sum(product, axis=0, keepdims=True)
                score_back = ((product - share * total) * SCALE).astype(LOW)
                value_back += dot_nn(low, grads * masks[h])
                key_back += dot_nn(score_back, query * masks[h])
                query_parts.append(dot_nn(key_t[32 * h : 32 * h + 32], score_back))
            query_back = jnp.concatenate(query_parts, axis=0).T
            projected_back[rows, 128 * t : 128 * t + 128] = query_back.astype(LOW)
            projected_back[rows, 512 + 128 * t : 640 + 128 * t] = key_back.astype(LOW)
            projected_back[rows, 1024 + 128 * t : 1152 + 128 * t] = value_back.astype(LOW)
    normed, inverse_std = normalize(windows[...].astype(WIDE))
    normed_low = normed.astype(LOW)
    for j in range(4):
        inward_t[384 * j : 384 * j + 384] = dot_tn(projected_back[:, 384 * j : 384 * j + 384], normed_low).astype(LOW)
    outward_t[...] = dot_tn(upstream_low, attended[...]).astype(LOW)
    mine = core[0]
    for place in range(16):
        for terms, parity in ((kept, mine), (sent, 1 - mine)):
            at = 2 * place + parity
            for k in range(4):
                lanes = slice(128 * k, 128 * k + 128)
                head = pl.ds(pl.multiple_of(48 * at, 16), 32)
                tail = pl.ds(pl.multiple_of(48 * at + 32, 16), 16)
                last = pl.ds(pl.multiple_of(16 * at, 16), 16)
                terms[place // 8, k, 0, place % 8] = inward_t[head, lanes]
                terms[place // 8, k, 1, place % 8, 0:16] = inward_t[tail, lanes]
                terms[place // 8, k, 1, place % 8, 16:32] = outward_t[last, lanes]
    loads[2].wait()
    normed_back = dot_nt(projected_back[...], inward[...])
    branch = inverse_std * (
        normed_back
        - jnp.mean(normed_back, axis=-1, keepdims=True)
        - normed * jnp.mean(normed_back * normed, axis=-1, keepdims=True)
    )
    result = (upstream + branch.astype(LOW).astype(WIDE)).astype(LOW)
    token_grads[...] = gather(table, FROM_WINDOWS, {0: result}).astype(LOW)


def shares_kernel(shares, inward_grads, outward_grads, merging_grads):
    for k in range(4):
        lanes = slice(128 * k, 128 * k + 128)
        inward_grads[0:32, lanes] = shares[2 * k, :, :128].astype(WIDE)
        inward_grads[32:48, lanes] = shares[2 * k + 1, 0:16, :128].astype(WIDE)
        outward_grads[:, lanes] = shares[2 * k + 1, 16:32, :128].astype(WIDE)
        for g in range(2):
            for half in range(2):
                at = 512 * k + 256 * half
                part = shares[2 * k + g, 16 * half : 16 * half + 16, 128:]
                merging_grads[16 * g : 16 * g + 16, at : at + 256] = part.astype(WIDE)


def planes_kernel(parts, kept, came, planes):
    total = parts[0].astype(WIDE)
    for k in range(1, 16):
        total += parts[k].astype(WIDE)
    planes[:, :, :128] = total.astype(LOW)
    for k in range(8):
        rows = slice(32 * k, 32 * k + 32)
        planes[k, :, 128:] = (kept[rows].astype(WIDE) + came[rows].astype(WIDE)).astype(LOW)


def share_kernel(parts, copies):
    total = parts[0].astype(WIDE)
    for k in range(1, 8):
        total += parts[k].astype(WIDE)
    total = total.astype(LOW)
    for k in range(8):
        copies[k] = total


def call(kernel, outs, *operands, scratch=(), scalars=0, room=8, far=(), far_outs=()):
    specs = [pl.BlockSpec()] * len(operands)
    for at in range(scalars):
        specs[at] = pl.BlockSpec(memory_space=pltpu.SMEM)
    for at in far:
        specs[at] = pl.BlockSpec(memory_space=pltpu.HBM)
    out_specs = [pl.BlockSpec(memory_space=pltpu.HBM) if at in far_outs else pl.BlockSpec() for at in range(len(outs))]
    return pl.pallas_call(
        kernel,
        in_specs=specs,
        out_specs=out_specs,
        out_shape=[
            jax.ShapeDtypeStruct(shape[:-1], WIDE) if shape[-1] is WIDE else jax.ShapeDtypeStruct(shape, LOW)
            for shape in outs
        ],
        scratch_shapes=[pltpu.VMEM(shape, LOW) if isinstance(shape, tuple) else shape for shape in scratch],
        compiler_params=pltpu.CompilerParams(vmem_limit_bytes=room * 1024 * 1024),
    )(*operands)


def from_behind(value, axis, steps):
    count = lax.axis_size(axis)
    pairs = [(source, (source + steps) % count) for source in range(count)]
    return lax.ppermute(value, axis, pairs)


def local_windows(layout):
    return layout.reshape(2, 6, 2, 12).transpose(2, 0, 1, 3).reshape(2, 144)


def to_neighbours(parts, steps):
    grp, lat, both = parts
    pairs = [
        (4 * 0 + 2 * row + level, (row + steps) % 4 * 2 + (level + steps) % 2) for row in range(4) for level in range(2)
    ]
    return (
        from_behind(grp, ("grp",), steps),
        from_behind(lat, ("lat",), steps),
        lax.ppermute(both, ("lat", "grp"), pairs),
    )


PLANES = [(120, 512), (96, 512), (96, 512)]


def shift_forward(table, tokens, cells):
    parts = to_neighbours(call(planes_in_kernel, PLANES, tokens, cells), -1)
    (columns,) = call(columns_in_kernel, [(108, 512)], tokens, cells, *parts)
    return (*parts, from_behind(columns, LON, -1))


def over_planes(terms):
    terms = terms.reshape((16,) + terms.shape[3:])
    return lax.all_to_all(terms, ("xh", "lat", "grp"), 0, 0)


def tied(*values):
    return lax.optimization_barrier(values)


def body(fine_tokens, region_ids, inward_weight, outward_weight, merging_weight, coarse_cotangent):
    table = jnp.asarray(TABLE)
    core = lax.axis_index("core").reshape(1)
    tokens = fine_tokens.reshape(288, 512)
    cells = coarse_cotangent.reshape(72, 1024)
    parts = shift_forward(table, tokens, cells)
    labels = local_windows(region_ids)
    block, last_row, windows, projected, attention, attended, shifted, columns, sent_columns = call(
        forward_kernel,
        [
            (288, 512), (48, 512), (288, 512), (288, 1536), (2, HEADS, 144, 144), (288, 512),
            (72, 1024), (2, 72, 256), (2, 72, 256),
        ],
        core, table, tokens, cells, *parts, labels.reshape(2, 1, 144), labels.reshape(2, 144, 1), inward_weight, outward_weight,
        scratch=[
            (512, 1536), (512, 512), (2, HEADS, 144, 144), (1024, 72), (256, 72),
            pltpu.SemaphoreType.DMA((2,)), pltpu.SemaphoreType.DMA((2, 4)),
        ],
        scalars=1, room=54, far=(10, 11), far_outs=(4,),
    )
    prior = from_behind(last_row, ("lat",), 1)
    other_columns = from_behind(sent_columns, ("core",), 1)
    merged_upstream = dot_nt(shifted, merging_weight)
    merged_normed, bundle, back, back_row = call(
        merge_kernel,
        [(72, 2048), (8, 4, 72, 256), (288, 512), (48, 512)],
        table, block, prior, merged_upstream, columns, other_columns,
    )
    next_row = from_behind(back_row, ("lat",), -1)
    next_row, bundle = tied(next_row, bundle)
    bundle = lax.all_to_all(bundle, ("lat", "grp"), 0, 0)
    token_grads, kept, sent = call(
        backward_kernel,
        [(288, 512), (2, 4, 2, 8, 32, 128), (2, 4, 2, 8, 32, 128)],
        core, table, back, next_row, windows, projected, attention, attended, inward_weight, outward_weight,
        scratch=[
            (288, 1536), (1536, 512), (512, 512), (2, HEADS, 144, 144), (512, 1536),
            pltpu.SemaphoreType.DMA((2,)), pltpu.SemaphoreType.DMA,
        ],
        scalars=1, room=54, far=(6, 8),
    )
    merged_normed, token_grads = tied(merged_normed, token_grads)
    coarse_field = dot_nn(merged_normed, merging_weight).astype(LOW)
    kept, sent, bundle, coarse_field = tied(kept, sent, bundle, coarse_field)
    came = from_behind(sent, ("core",), 1)
    block_terms = (kept.astype(WIDE) + came.astype(WIDE)).astype(LOW)
    block_planes = over_planes(block_terms)
    other_normed = from_behind(bundle[:, 2:], ("core",), 1)
    merging_kept, merging_sent = call(
        merging_kernel,
        [(256, 256), (256, 256)],
        lax.axis_index("xh").reshape(1), bundle, other_normed,
        scratch=[(512, 256)], scalars=1,
    )
    merging_came = from_behind(merging_sent, ("xh",), 1)
    (lon_out,) = call(columns_out_kernel, [(108, 512)], table, token_grads, coarse_field)
    lon_out = from_behind(lon_out, LON, 1)
    parts_out = call(planes_out_kernel, PLANES, table, token_grads, coarse_field, lon_out)
    block_planes, merging_came, *parts_out = tied(block_planes, merging_came, *parts_out)
    parts_out = to_neighbours(parts_out, 1)
    (planes,) = call(planes_kernel, [(8, 32, 384)], block_planes, merging_kept, merging_came)
    (share,) = call(share_kernel, [(8, 32, 384)], lax.all_to_all(planes, ("z",), 0, 0))
    share, *parts_out = tied(share, *parts_out)
    shares = lax.all_to_all(share, ("lat", "grp"), 0, 0)
    token_grads, coarse_field = call(
        all_out_kernel, [(288, 512), (72, 1024)], table, token_grads, coarse_field, *parts_out, lon_out
    )
    grads = call(shares_kernel, [(48, 512, WIDE), (16, 512, WIDE), (32, 2048, WIDE)], shares)
    return (
        coarse_field.reshape(2, 3, 12, 1024),
        token_grads.reshape(2, 6, 24, 512),
        *(share.T for share in grads),
    )


def solution(mesh):
    fine = Mesh(mesh.devices.reshape(4, 2, 8, 2, 2), ("lat", "xh", "z", "core", "grp"))
    return jax.shard_map(
        body,
        mesh=fine,
        in_specs=(
            P("grp", "lat", LON, None),
            P("grp", "lat", LON),
            P(),
            P(),
            P(),
            P("grp", "lat", LON, None),
        ),
        out_specs=(
            P("grp", "lat", LON, None),
            P("grp", "lat", LON, None),
            P(None, LON),
            P(None, LON),
            P(None, LON),
        ),
        check_vma=False,
    )
```

```python
import jax
import jax.numpy as jnp
import numpy as np
from jax import lax
from jax.experimental import pallas as pl
from jax.experimental.pallas import tpu as pltpu
from jax.sharding import Mesh, PartitionSpec as P

HEADS = 16
LON = ("xh", "z", "core")
SCALE = 32 ** (-0.5)
LOW = jnp.bfloat16
WIDE = jnp.float32


def halves(fields):
    return np.concatenate([fields.reshape(-1), (fields + 1000).reshape(-1)])


def join(*parts):
    return np.concatenate([part.reshape(-1) for part in parts])


FINE_AT = np.arange(288).reshape(2, 6, 24)
CELL_AT = 1000 + np.arange(72).reshape(2, 3, 12)


def arrived(source, rows):
    fine = 1000 * source + np.arange(72).reshape(3, 24)
    cells = 1000 * source + 72 + np.arange(12 * rows).reshape(rows, 12)
    return fine, cells, 12 * rows


def shift_in():
    grp, lat, both = arrived(3, 2), arrived(4, 1), arrived(5, 1)
    first = [
        join(FINE_AT[0, 3:], halves(CELL_AT[0, 1:])),
        join(FINE_AT[1, :3], halves(CELL_AT[1, :1])),
        join(FINE_AT[0, :3], halves(CELL_AT[0, :1])),
    ]
    fine = np.stack([np.concatenate([FINE_AT[1, 3:], lat[0]]), np.concatenate([grp[0], both[0]])])
    left = np.stack([np.concatenate([CELL_AT[1, 1:], lat[1]]), np.concatenate([grp[1], both[1]])])
    right = np.stack(
        [np.concatenate([CELL_AT[1, 1:] + 1000, lat[1] + lat[2]]), np.concatenate([grp[1] + grp[2], both[1] + both[2]])]
    )
    second = join(fine[:, :, :6], left[:, :, :3], right[:, :, :3])
    lon_fine = 6000 + np.arange(72).reshape(2, 6, 6)
    lon_cells = 6072 + np.arange(18).reshape(2, 3, 3)
    fine = np.concatenate([fine[:, :, 6:], lon_fine], axis=2)
    left = np.concatenate([left[:, :, 3:], lon_cells], axis=2)
    right = np.concatenate([right[:, :, 3:], lon_cells + 18], axis=2)
    windows = fine.reshape(2, 6, 2, 12).transpose(2, 0, 1, 3)
    return join(*first), second, windows.reshape(-1), join(left, right)


def shift_out():
    first = join(FINE_AT[:, :, 18:], CELL_AT[:, :, 9:], CELL_AT[:, :, 9:] + 1000)
    lon_fine = 6000 + np.arange(72).reshape(2, 6, 6)
    lon_cells = 6072 + np.arange(18).reshape(2, 3, 3)
    fine = np.concatenate([lon_fine, FINE_AT[:, :, :18]], axis=2)
    left = np.concatenate([lon_cells, CELL_AT[:, :, :9]], axis=2)
    right = np.concatenate([lon_cells + 18, CELL_AT[:, :, :9] + 1000], axis=2)
    second = join(
        fine[1, :3], left[1, :2], right[1, :2], fine[0, 3:], left[0, 2], right[0, 2], fine[1, 3:], left[1, 2], right[1, 2]
    )
    grp, lat, both = arrived(3, 2), arrived(4, 1), arrived(5, 1)
    fine = np.stack([np.concatenate([both[0], grp[0]]), np.concatenate([lat[0], fine[0, :3]])])
    left = np.stack([np.concatenate([both[1], grp[1]]), np.concatenate([lat[1], left[0, :2]])])
    right = np.stack(
        [np.concatenate([both[1] + both[2], grp[1] + grp[2]]), np.concatenate([lat[1] + lat[2], right[0, :2]])]
    )
    return first, second, join(fine, left, right)


def block_maps():
    natural = np.arange(288).reshape(2, 6, 24)
    windows = natural.reshape(2, 6, 2, 12).transpose(2, 0, 1, 3).reshape(288)
    extended = np.concatenate([1000 + np.arange(48).reshape(2, 1, 24), natural[:, :5]], axis=1)
    to_cells = extended.reshape(2, 3, 2, 12, 2).transpose(4, 2, 0, 1, 3).reshape(288)
    from_cells = np.full(336, -1)
    from_cells[np.where(to_cells < 1000, to_cells, to_cells - 712)] = np.arange(288)
    replaced = natural.copy()
    replaced[:, 5] = 1000 + np.arange(48).reshape(2, 24)
    return np.argsort(windows), to_cells, from_cells, replaced.reshape(288)[windows]


def row_table():
    columns = [*shift_in(), *shift_out(), *block_maps()]
    table = np.full((432, len(columns)), -1, np.int32)
    for at, column in enumerate(columns):
        table[: len(column), at] = column
    return table


TABLE = row_table()
(
    IN_FIRST, IN_SECOND, IN_WINDOWS, IN_CELLS, OUT_FIRST, OUT_SECOND, OUT_ALL,
    FROM_WINDOWS, TO_CELLS, FROM_CELLS, UPSTREAM,
) = range(11)
ROWS = [int((TABLE[:, at] >= 0).sum()) for at in range(11)]
ROWS[FROM_CELLS] = 336


def gather(table, column, sources):
    return gather_named(table[: ROWS[column], column : column + 1], sources)


def gather_named(names, sources):
    total = 0.0
    for source, value in sources.items():
        place = lax.broadcasted_iota(jnp.int32, (names.shape[0], value.shape[0]), 1) + 1000 * source
        total += dot_nn((names == place).astype(WIDE).astype(LOW), value)
    return total


def dot_nn(a, b):
    return lax.dot_general(a, b, (((1,), (0,)), ((), ())), preferred_element_type=WIDE)


def dot_nt(a, b):
    return lax.dot_general(a, b, (((1,), (1,)), ((), ())), preferred_element_type=WIDE)


def dot_tn(a, b):
    return lax.dot_general(a, b, (((0,), (0,)), ((), ())), preferred_element_type=WIDE)


def head_masks():
    head = lax.broadcasted_iota(jnp.int32, (144, 128), 1) >> 5
    return [(head == h).astype(WIDE).astype(LOW) for h in range(4)]


def normalize(values):
    centred = values - jnp.mean(values, axis=-1, keepdims=True)
    inverse_std = lax.rsqrt(jnp.mean(centred * centred, axis=-1, keepdims=True) + 1e-05)
    return (centred * inverse_std, inverse_std)


def own(tokens, cells):
    return {0: tokens[...], 1: cells[:, :512], 2: cells[:, 512:]}


def arrivals(grp, lat, both):
    return {3: grp[...], 4: lat[...], 5: both[...]}


def store_planes(packed, grp, lat, both):
    grp[...] = packed[:120].astype(LOW)
    lat[...] = packed[120:216].astype(LOW)
    both[...] = packed[216:].astype(LOW)


def runs(target):
    target = np.asarray(target)
    begins = [0] + [at for at in range(1, len(target)) if target[at] != target[at - 1] + 1]
    return [(at, int(target[at]) - at) for at in begins]


def column_names(column):
    row = lax.broadcasted_iota(jnp.int32, (ROWS[column], 1), 0)
    ahead = jnp.zeros_like(row)
    for begin, difference in runs(TABLE[: ROWS[column], column]):
        ahead = jnp.where(row >= begin, difference, ahead)
    return row + ahead


def planes_in_kernel(tokens, cells, *outs):
    store_planes(gather_named(column_names(IN_FIRST), own(tokens, cells)), *outs)


def columns_in_kernel(tokens, cells, grp, lat, both, out):
    sources = own(tokens, cells) | arrivals(grp, lat, both)
    out[...] = gather_named(column_names(IN_SECOND), sources).astype(LOW)


def columns_out_kernel(table, tokens, cells, out):
    out[...] = gather(table, OUT_FIRST, own(tokens, cells)).astype(LOW)


def planes_out_kernel(table, tokens, cells, lon, *outs):
    store_planes(gather(table, OUT_SECOND, own(tokens, cells) | {6: lon[...]}), *outs)


def all_out_kernel(table, tokens, cells, grp, lat, both, lon, fine, coarse):
    packed = gather(table, OUT_ALL, own(tokens, cells) | arrivals(grp, lat, both) | {6: lon[...]})
    fine[...] = packed[:288].astype(LOW)
    coarse[:, :512] = packed[288:360].astype(LOW)
    coarse[:, 512:] = packed[360:].astype(LOW)


def shift_cotangent(core, table, sources, shifted, kept, sent, columns, picked):
    packed = gather(table, IN_CELLS, sources)
    cotangent = jnp.concatenate([packed[:72], packed[72:]], axis=1)
    shifted[...] = cotangent.astype(LOW)
    columns[...] = cotangent.T.astype(LOW)
    for out, parity in ((kept, core[0]), (sent, 1 - core[0])):
        for g in range(2):
            for m in range(16):
                at = pl.multiple_of(64 * m + 32 * parity + 16 * g, 16)
                picked[16 * m : 16 * m + 16] = columns[pl.ds(at, 16)]
            out[g] = picked[...].astype(WIDE).T.astype(LOW)


def forward_kernel(
    core, table, tokens, cells, grp, lat, both, lon, row_labels, column_labels, far_inward, far_outward,
    block, last_row, windows, projected, far_attention, attended, shifted, kept, sent,
    inward, outward, attention, columns, picked, weights_in, shares_out,
):
    fetches = [
        pltpu.make_async_copy(far_inward, inward, weights_in.at[0]),
        pltpu.make_async_copy(far_outward, outward, weights_in.at[1]),
    ]
    for copy in fetches:
        copy.start()
    stores = []
    arrived_parts = arrivals(grp, lat, both) | {6: lon[...]}
    values = gather(table, IN_WINDOWS, {0: tokens[...]} | arrived_parts)
    windows[...] = values.astype(LOW)
    normed = normalize(values)[0].astype(LOW)
    fetches[0].wait()
    projected[...] = dot_nn(normed, inward[...]).astype(LOW)
    masks = head_masks()
    for w in range(2):
        rows = slice(144 * w, 144 * w + 144)
        allowed = column_labels[w] == row_labels[w]
        for t in range(4):
            query = projected[rows, 128 * t : 128 * t + 128]
            key = projected[rows, 512 + 128 * t : 640 + 128 * t]
            value_t = projected[rows, 1024 + 128 * t : 1152 + 128 * t].T
            parts = []
            for h in range(4):
                scores = dot_nt(key * masks[h], query) * SCALE
                scores = jnp.where(allowed, scores, -1e30)
                weights = jnp.exp(scores - jnp.max(scores, axis=0, keepdims=True))
                share = weights * (1.0 / jnp.sum(weights, axis=0, keepdims=True))
                share = share.astype(LOW)
                attention[w, 4 * t + h] = share
                parts.append(dot_nn(value_t[32 * h : 32 * h + 32], share))
            attended[rows, 128 * t : 128 * t + 128] = jnp.concatenate(parts, axis=0).T.astype(LOW)
            heads = pl.ds(4 * t, 4)
            store = pltpu.make_async_copy(attention.at[w, heads], far_attention.at[w, heads], shares_out.at[w, t])
            store.start()
            stores.append(store)
    fetches[1].wait()
    result = (values + dot_nn(attended[...], outward[...])).astype(LOW)
    natural = gather(table, FROM_WINDOWS, {0: result})
    block[...] = natural.astype(LOW)
    last_row[...] = jnp.concatenate([natural[120:144], natural[264:]], axis=0).astype(LOW)
    cell_parts = {1: cells[:, :512], 2: cells[:, 512:]} | arrived_parts
    shift_cotangent(core, table, cell_parts, shifted, kept, sent, columns, picked)
    for store in stores:
        store.wait()


def merge_kernel(table, block, prior, upstream, columns, other_columns, normed, bundle, back, back_row):
    merged = gather(table, TO_CELLS, {0: block[...], 1: prior[...]})
    pieces = [merged[72 * k : 72 * k + 72] for k in range(4)]
    exact, inverse_std = normalize(jnp.concatenate(pieces, axis=1))
    normed[...] = exact.astype(LOW)
    for k in range(8):
        bundle[k, 0] = columns[k % 2]
        bundle[k, 1] = other_columns[k % 2]
        for half in range(2):
            at = 512 * (k // 2) + 256 * half
            bundle[k, 2 + half] = exact[:, at : at + 256].astype(LOW)
    grads = upstream[...]
    grads = inverse_std * (
        grads
        - jnp.mean(grads, axis=-1, keepdims=True)
        - exact * jnp.mean(grads * exact, axis=-1, keepdims=True)
    )
    stacked = jnp.concatenate([grads[:, 512 * k : 512 * k + 512] for k in range(4)], axis=0)
    stacked = stacked.astype(LOW)
    positions = gather(table, FROM_CELLS, {0: stacked})
    back[...] = positions[:288].astype(LOW)
    back_row[...] = positions[288:].astype(LOW)


def merging_kernel(xh, bundle, other_normed, kept, sent, total):
    for half in range(2):
        terms = 0.0
        for k in range(8):
            terms += dot_tn(bundle[k, 0], bundle[k, 2 + half]) + dot_tn(bundle[k, 1], other_normed[k, half])
        terms = terms.astype(LOW)
        for m in range(16):
            total[32 * m + 16 * half : 32 * m + 16 * half + 16] = terms[16 * m : 16 * m + 16]
    kept[...] = total[pl.ds(pl.multiple_of(256 * xh[0], 256), 256)]
    sent[...] = total[pl.ds(pl.multiple_of(256 - 256 * xh[0], 256), 256)]


def backward_kernel(
    core, table, back, next_row, windows, projected, far_attention, attended, far_inward, outward,
    token_grads, kept, sent, projected_back, inward_t, outward_t, attention, inward, shares_in, weight_in,
):
    loads = [pltpu.make_async_copy(far_attention.at[w], attention.at[w], shares_in.at[w]) for w in range(2)]
    loads.append(pltpu.make_async_copy(far_inward, inward, weight_in))
    for load in loads:
        load.start()
    upstream = gather(table, UPSTREAM, {0: back[...], 1: next_row[...]})
    upstream_low = upstream.astype(LOW)
    attended_back = dot_nt(upstream_low, outward[...]).astype(LOW)
    masks = head_masks()
    for w in range(2):
        rows = slice(144 * w, 144 * w + 144)
        loads[w].wait()
        for t in range(4):
            query = projected[rows, 128 * t : 128 * t + 128]
            key_t = projected[rows, 512 + 128 * t : 640 + 128 * t].T
            value = projected[rows, 1024 + 128 * t : 1152 + 128 * t]
            grads = attended_back[rows, 128 * t : 128 * t + 128]
            query_parts, key_back, value_back = [], 0.0, 0.0
            for h in range(4):
                low = attention[w, 4 * t + h]
                share = low.astype(WIDE)
                product = share * dot_nt(value * masks[h], grads)
                total = jnp.sum(product, axis=0, keepdims=True)
                score_back = ((product - share * total) * SCALE).astype(LOW)
                value_back += dot_nn(low, grads * masks[h])
                key_back += dot_nn(score_back, query * masks[h])
                query_parts.append(dot_nn(key_t[32 * h : 32 * h + 32], score_back))
            query_back = jnp.concatenate(query_parts, axis=0).T
            projected_back[rows, 128 * t : 128 * t + 128] = query_back.astype(LOW)
            projected_back[rows, 512 + 128 * t : 640 + 128 * t] = key_back.astype(LOW)
            projected_back[rows, 1024 + 128 * t : 1152 + 128 * t] = value_back.astype(LOW)
    normed, inverse_std = normalize(windows[...].astype(WIDE))
    normed_low = normed.astype(LOW)
    for j in range(4):
        inward_t[384 * j : 384 * j + 384] = dot_tn(projected_back[:, 384 * j : 384 * j + 384], normed_low).astype(LOW)
    outward_t[...] = dot_tn(upstream_low, attended[...]).astype(LOW)
    mine = core[0]
    for place in range(16):
        for terms, parity in ((kept, mine), (sent, 1 - mine)):
            at = 2 * place + parity
            for k in range(4):
                lanes = slice(128 * k, 128 * k + 128)
                head = pl.ds(pl.multiple_of(48 * at, 16), 32)
                tail = pl.ds(pl.multiple_of(48 * at + 32, 16), 16)
                last = pl.ds(pl.multiple_of(16 * at, 16), 16)
                terms[place // 8, k, 0, place % 8] = inward_t[head, lanes]
                terms[place // 8, k, 1, place % 8, 0:16] = inward_t[tail, lanes]
                terms[place // 8, k, 1, place % 8, 16:32] = outward_t[last, lanes]
    loads[2].wait()
    normed_back = dot_nt(projected_back[...], inward[...])
    branch = inverse_std * (
        normed_back
        - jnp.mean(normed_back, axis=-1, keepdims=True)
        - normed * jnp.mean(normed_back * normed, axis=-1, keepdims=True)
    )
    result = (upstream + branch.astype(LOW).astype(WIDE)).astype(LOW)
    token_grads[...] = gather(table, FROM_WINDOWS, {0: result}).astype(LOW)


def shares_kernel(shares, inward_grads, outward_grads, merging_grads):
    for k in range(4):
        lanes = slice(128 * k, 128 * k + 128)
        inward_grads[0:32, lanes] = shares[2 * k, :, :128].astype(WIDE)
        inward_grads[32:48, lanes] = shares[2 * k + 1, 0:16, :128].astype(WIDE)
        outward_grads[:, lanes] = shares[2 * k + 1, 16:32, :128].astype(WIDE)
        for g in range(2):
            for half in range(2):
                at = 512 * k + 256 * half
                part = shares[2 * k + g, 16 * half : 16 * half + 16, 128:]
                merging_grads[16 * g : 16 * g + 16, at : at + 256] = part.astype(WIDE)


def planes_kernel(parts, kept, came, planes):
    total = parts[0].astype(WIDE)
    for k in range(1, 16):
        total += parts[k].astype(WIDE)
    planes[:, :, :128] = total.astype(LOW)
    for k in range(8):
        rows = slice(32 * k, 32 * k + 32)
        planes[k, :, 128:] = (kept[rows].astype(WIDE) + came[rows].astype(WIDE)).astype(LOW)


def share_kernel(parts, copies):
    total = parts[0].astype(WIDE)
    for k in range(1, 8):
        total += parts[k].astype(WIDE)
    total = total.astype(LOW)
    for k in range(8):
        copies[k] = total


def call(kernel, outs, *operands, scratch=(), scalars=0, room=8, far=(), far_outs=()):
    specs = [pl.BlockSpec()] * len(operands)
    for at in range(scalars):
        specs[at] = pl.BlockSpec(memory_space=pltpu.SMEM)
    for at in far:
        specs[at] = pl.BlockSpec(memory_space=pltpu.HBM)
    out_specs = [pl.BlockSpec(memory_space=pltpu.HBM) if at in far_outs else pl.BlockSpec() for at in range(len(outs))]
    return pl.pallas_call(
        kernel,
        in_specs=specs,
        out_specs=out_specs,
        out_shape=[
            jax.ShapeDtypeStruct(shape[:-1], WIDE) if shape[-1] is WIDE else jax.ShapeDtypeStruct(shape, LOW)
            for shape in outs
        ],
        scratch_shapes=[pltpu.VMEM(shape, LOW) if isinstance(shape, tuple) else shape for shape in scratch],
        compiler_params=pltpu.CompilerParams(vmem_limit_bytes=room * 1024 * 1024),
    )(*operands)


def from_behind(value, axis, steps):
    count = lax.axis_size(axis)
    pairs = [(source, (source + steps) % count) for source in range(count)]
    return lax.ppermute(value, axis, pairs)


def local_windows(layout):
    return layout.reshape(2, 6, 2, 12).transpose(2, 0, 1, 3).reshape(2, 144)


def to_neighbours(parts, steps):
    grp, lat, both = parts
    pairs = [
        (4 * 0 + 2 * row + level, (row + steps) % 4 * 2 + (level + steps) % 2) for row in range(4) for level in range(2)
    ]
    return (
        from_behind(grp, ("grp",), steps),
        from_behind(lat, ("lat",), steps),
        lax.ppermute(both, ("lat", "grp"), pairs),
    )


PLANES = [(120, 512), (96, 512), (96, 512)]


def shift_forward(table, tokens, cells):
    parts = to_neighbours(call(planes_in_kernel, PLANES, tokens, cells), -1)
    (columns,) = call(columns_in_kernel, [(108, 512)], tokens, cells, *parts)
    return (*parts, from_behind(columns, LON, -1))


def over_planes(terms):
    terms = terms.reshape((16,) + terms.shape[3:])
    return lax.all_to_all(terms, ("xh", "lat", "grp"), 0, 0)


def tied(*values):
    return lax.optimization_barrier(values)


def body(fine_tokens, region_ids, inward_weight, outward_weight, merging_weight, coarse_cotangent):
    table = jnp.asarray(TABLE)
    core = lax.axis_index("core").reshape(1)
    tokens = fine_tokens.reshape(288, 512)
    cells = coarse_cotangent.reshape(72, 1024)
    parts = shift_forward(table, tokens, cells)
    labels = local_windows(region_ids)
    block, last_row, windows, projected, attention, attended, shifted, columns, sent_columns = call(
        forward_kernel,
        [
            (288, 512), (48, 512), (288, 512), (288, 1536), (2, HEADS, 144, 144), (288, 512),
            (72, 1024), (2, 72, 256), (2, 72, 256),
        ],
        core, table, tokens, cells, *parts, labels.reshape(2, 1, 144), labels.reshape(2, 144, 1), inward_weight, outward_weight,
        scratch=[
            (512, 1536), (512, 512), (2, HEADS, 144, 144), (1024, 72), (256, 72),
            pltpu.SemaphoreType.DMA((2,)), pltpu.SemaphoreType.DMA((2, 4)),
        ],
        scalars=1, room=54, far=(10, 11), far_outs=(4,),
    )
    prior = from_behind(last_row, ("lat",), 1)
    other_columns = from_behind(sent_columns, ("core",), 1)
    merged_upstream = dot_nt(shifted, merging_weight)
    merged_normed, bundle, back, back_row = call(
        merge_kernel,
        [(72, 2048), (8, 4, 72, 256), (288, 512), (48, 512)],
        table, block, prior, merged_upstream, columns, other_columns,
    )
    next_row = from_behind(back_row, ("lat",), -1)
    next_row, bundle = tied(next_row, bundle)
    bundle = lax.all_to_all(bundle, ("lat", "grp"), 0, 0)
    token_grads, kept, sent = call(
        backward_kernel,
        [(288, 512), (2, 4, 2, 8, 32, 128), (2, 4, 2, 8, 32, 128)],
        core, table, back, next_row, windows, projected, attention, attended, inward_weight, outward_weight,
        scratch=[
            (288, 1536), (1536, 512), (512, 512), (2, HEADS, 144, 144), (512, 1536),
            pltpu.SemaphoreType.DMA((2,)), pltpu.SemaphoreType.DMA,
        ],
        scalars=1, room=54, far=(6, 8),
    )
    merged_normed, token_grads = tied(merged_normed, token_grads)
    coarse_field = dot_nn(merged_normed, merging_weight).astype(LOW)
    kept, sent, bundle, coarse_field = tied(kept, sent, bundle, coarse_field)
    came = from_behind(sent, ("core",), 1)
    block_terms = (kept.astype(WIDE) + came.astype(WIDE)).astype(LOW)
    other_normed = from_behind(bundle[:, 2:], ("core",), 1)
    block_terms, other_normed = tied(block_terms, other_normed)
    block_planes = over_planes(block_terms)
    merging_kept, merging_sent = call(
        merging_kernel,
        [(256, 256), (256, 256)],
        lax.axis_index("xh").reshape(1), bundle, other_normed,
        scratch=[(512, 256)], scalars=1,
    )
    merging_came = from_behind(merging_sent, ("xh",), 1)
    (lon_out,) = call(columns_out_kernel, [(108, 512)], table, token_grads, coarse_field)
    lon_out = from_behind(lon_out, LON, 1)
    parts_out = call(planes_out_kernel, PLANES, table, token_grads, coarse_field, lon_out)
    block_planes, merging_came, *parts_out = tied(block_planes, merging_came, *parts_out)
    parts_out = to_neighbours(parts_out, 1)
    (planes,) = call(planes_kernel, [(8, 32, 384)], block_planes, merging_kept, merging_came)
    (share,) = call(share_kernel, [(8, 32, 384)], lax.all_to_all(planes, ("z",), 0, 0))
    share, *parts_out = tied(share, *parts_out)
    shares = lax.all_to_all(share, ("lat", "grp"), 0, 0)
    token_grads, coarse_field = call(
        all_out_kernel, [(288, 512), (72, 1024)], table, token_grads, coarse_field, *parts_out, lon_out
    )
    grads = call(shares_kernel, [(48, 512, WIDE), (16, 512, WIDE), (32, 2048, WIDE)], shares)
    return (
        coarse_field.reshape(2, 3, 12, 1024),
        token_grads.reshape(2, 6, 24, 512),
        *(share.T for share in grads),
    )


def solution(mesh):
    fine = Mesh(mesh.devices.reshape(4, 2, 8, 2, 2), ("lat", "xh", "z", "core", "grp"))
    return jax.shard_map(
        body,
        mesh=fine,
        in_specs=(
            P("grp", "lat", LON, None),
            P("grp", "lat", LON),
            P(),
            P(),
            P(),
            P("grp", "lat", LON, None),
        ),
        out_specs=(
            P("grp", "lat", LON, None),
            P("grp", "lat", LON, None),
            P(None, LON),
            P(None, LON),
            P(None, LON),
        ),
        check_vma=False,
    )
```
